32 devices in a mesh: expert: 4 (over x, core), fsdp: 8 (over z, y).
Axes of the slice: x: 2, y: 2, z: 4, core: 2. Of those that a mesh axis runs over, the one named last changes fastest.
Arguments:
- tokens: bfloat16 [4096, 1536], P(('expert', 'fsdp')), may hold values from -6 to 6
- gate_probs: float32 [4096, 2], P(('expert', 'fsdp')), may hold values from 0.1 to 1
- expert_ids: int32 [4096, 2], P(('expert', 'fsdp')), may hold values from 0 to 3, all different within a row; in each aligned block of 128 rows (0 to 127, 128 to 255, ...) at most 64 rows name the same one
- cotangent: bfloat16 [4096, 1536], P(('expert', 'fsdp')), may hold values from -0.59765625 to 0.59765625
- gate_weight: bfloat16 [4, 1536, 2048], P('expert', None, 'fsdp'), may hold values from -0.15625 to 0.15625
- up_weight: bfloat16 [4, 1536, 2048], P('expert', None, 'fsdp'), may hold values from -0.15625 to 0.15625
- down_weight: bfloat16 [4, 2048, 1536], P('expert', 'fsdp'), may hold values from -0.125 to 0.125
Outputs:
- mixed: bfloat16 [4096, 1536], P(('expert', 'fsdp'))
- d_tokens: bfloat16 [4096, 1536], P(('expert', 'fsdp'))
- d_gates: float32 [4096, 2], P(('expert', 'fsdp'))
- d_gate_weight: float32 [4, 1536, 2048], P('expert', None, 'fsdp')
- d_up_weight: float32 [4, 1536, 2048], P('expert', None, 'fsdp')
- d_down_weight: float32 [4, 2048, 1536], P('expert', 'fsdp')
The draws below stay inside these ranges and needn't reach their ends.
Inputs may be any that keep to these rules, and one draw needn't show every extreme that they name: `expert_ids`: the two experts of a token differ. In the 128 rows of one device every expert is named exactly 64 times.
All inputs are finite; a program needn't handle non-finite values.
Results may differ from the reference program's by a relative error of at most 0.015.
Values may be sent and summed in bfloat16 or wider, within the bound.
No kernel may reach another device: no remote copies, remote signals or barrier semaphores. Data moves between devices by JAX's collectives and lax.ppermute only.
A program may use at most 192 MiB of HBM per device.

```python
import math
import jax
import jax.numpy as jnp
import numpy as np
from jax import lax

D = 1536
FF = 2048
TOK_DEV = 128
EXPERTS = 4
CAP = 64
TOKENS = 4096
N_FSDP = 8


def steps_of(stream_key, shape, split, low, largest):
    def one(axis_at, blocks):
        draws = jax.random.uniform(jax.random.fold_in(jax.random.fold_in(stream_key, 6), axis_at), (blocks,), jnp.float32, low / len(split), largest / len(split))
        return jnp.repeat(jnp.exp(draws), shape[axis_at] // blocks).reshape((-1,) + (1,) * (len(shape) - axis_at - 1))

    gain = one(*split[0])
    for cut in split[1:]:
        gain = gain * one(*cut)
    return gain


def assign_block(stream_key, own, number, rows, number_of, top, most, skew):
    ranking = jax.random.permutation(stream_key, number_of)
    packed, common = shares(number_of, rows * top, most, skew, True), shares(number_of, rows * top, most, skew, False)
    places = jnp.arange(number_of)

    def named(sizes, rotation):
        used = int((sizes > 0).sum())
        fixed = max(1, used // 4)
        moved = fixed + (places - fixed + rotation * (used - fixed)) % max(1, number_of - fixed)
        return jnp.zeros((number_of,), jnp.int32).at[ranking[jnp.where(places < fixed, places, moved)]].set(jnp.asarray(sizes, jnp.int32))

    sizes = jnp.where(number % 4 == 0, named(packed, number // 4), named(common, number - number // 4 - 1))
    mixed = jax.random.permutation(jax.random.fold_in(own, 3), number_of)
    donor, sink = mixed[0:number_of // 2 * 2:2], mixed[1:number_of // 2 * 2:2]
    margin = jnp.minimum(sizes[donor] - 1, most - sizes[sink]) // 2
    margin = jnp.where((donor == ranking[0]) | (sink == ranking[0]) | (sizes[sink] == 0), 0, jnp.maximum(margin, 0))
    moved = jax.random.randint(jax.random.fold_in(own, 4), (number_of // 2,), 0, 1 << 20) % (margin + 1)
    sizes = sizes.at[donor].add(-moved).at[sink].add(moved)
    members = jnp.searchsorted(jnp.cumsum(sizes), jnp.arange(rows * top), side="right").astype(jnp.int32)
    listing = members.reshape(top, rows).T
    listing = listing[jax.random.permutation(jax.random.fold_in(own, 1), rows)]
    rotation = jax.random.randint(jax.random.fold_in(own, 2), (rows, 1), 0, top)
    return jnp.take_along_axis(listing, (jnp.arange(top)[None, :] + rotation) % top, axis=1)


def shares(number_of, total, bound, slope, full):
    portions = [(1 << 20) // math.isqrt(grade ** slope) + 1 for grade in range(1, number_of + 1)]
    largest = bound if full else min(bound, max(-(-total // number_of), total * portions[0] // sum(portions)))
    least = 1 if total - largest >= number_of - 1 else 0
    given, spare = [largest] + [least] * (number_of - 1), total - largest - least * (number_of - 1)
    while spare > 0:
        movable = [i for i in range(1, number_of) if given[i] < largest] or [i for i in range(1, number_of) if given[i] < bound]
        mass, budget = sum([portions[i] for i in movable]), spare
        for i in movable:
            more = min(bound - given[i], max(1, budget * portions[i] // mass), spare)
            given[i] = given[i] + more
            spare = spare - more
    return np.array(given)


def centred(own_key, extent, width, bound, split=(), held_as=jnp.bfloat16):
    gain = steps_of(own_key, extent, split, -0.22, 0.18) if split else 1.0
    drawn = jax.random.normal(own_key, extent, jnp.float32) * width * gain
    return jnp.minimum(jnp.maximum(drawn, -bound), bound).astype(held_as)


def setup_inputs(seed: int = 0) -> dict:
    keys = jax.random.split(jax.random.key(seed), 8)
    tokens = centred(keys[0], (TOKENS, D), 1.0, 6.0, ((0, 32),))
    gate_probs = jnp.clip(0.1 + 0.9 * jax.random.uniform(keys[1], (TOKENS, 2), jnp.float32) ** steps_of(keys[1], (TOKENS, 2), ((0, 32),), -0.2, 0.2), 0.1, 1.0)
    expert_ids_keys = jax.random.split(jax.random.fold_in(keys[2], 1), TOKENS // TOK_DEV)
    expert_ids_turns = jax.random.permutation(jax.random.fold_in(keys[2], 3), TOKENS // TOK_DEV)
    expert_ids = jax.vmap(lambda own, number: assign_block(jax.random.fold_in(keys[2], 2), own, number, TOK_DEV, EXPERTS, 2, CAP, 0))(expert_ids_keys, expert_ids_turns).reshape((TOKENS, 2))
    cotangent = centred(keys[3], (TOKENS, D), 0.1, 0.59765625, ((0, 32),))
    gate_weight = centred(keys[4], (EXPERTS, D, FF), D ** -0.5, 0.15625, ((0, 4), (2, 8)))
    up_weight = centred(keys[5], (EXPERTS, D, FF), D ** -0.5, 0.15625, ((0, 4), (2, 8)))
    down_weight = centred(keys[6], (EXPERTS, FF, D), FF ** -0.5, 0.125, ((0, 4), (1, 8)))
    return dict(tokens=tokens, gate_probs=gate_probs, expert_ids=expert_ids, cotangent=cotangent, gate_weight=gate_weight, up_weight=up_weight, down_weight=down_weight)


def round_sum(parts):
    rounded = lax.optimization_barrier(parts.astype(jnp.bfloat16))
    return jnp.sum(rounded.astype(jnp.float32), axis=0).astype(jnp.bfloat16)


def reference(tokens, gate_probs, expert_ids, cotangent, gate_weight, up_weight, down_weight):
    dev_count = TOKENS // TOK_DEV
    pair_ids = expert_ids.reshape(dev_count, 2 * TOK_DEV)
    onehot = (pair_ids[:, :, None] == jnp.arange(EXPERTS, dtype=jnp.int32)[None, None, :]).astype(jnp.int32)
    before = jnp.cumsum(onehot, axis=1) - onehot
    slot_pos = jnp.sum(before * onehot, axis=2)
    row_pos = (jnp.arange(dev_count, dtype=jnp.int32)[:, None] * CAP + slot_pos).reshape(-1).astype(jnp.int32)
    flat_ids = expert_ids.reshape(-1).astype(jnp.int32)
    slot_rows = dev_count * CAP
    pair_index = jnp.arange(2 * TOKENS, dtype=jnp.int32)
    table = jnp.full((EXPERTS, slot_rows), 2 * TOKENS, jnp.int32).at[flat_ids, row_pos].set(pair_index)
    token_pad = jnp.concatenate([tokens, jnp.zeros((1, D), tokens.dtype)], axis=0)
    scaled = (gate_probs[:, :, None] * cotangent.astype(jnp.float32)[:, None, :]).astype(jnp.bfloat16)
    scaled_pad = jnp.concatenate([scaled.reshape(2 * TOKENS, D), jnp.zeros((1, D), jnp.bfloat16)], axis=0)
    shard = FF // N_FSDP

    def one_expert(operands):
        index, w_gate, w_up, w_down = operands
        rows_in = token_pad[index // 2]
        grad_rows = scaled_pad[index]
        pre_gate = jnp.dot(rows_in, w_gate, preferred_element_type=jnp.float32)
        pre_up = jnp.dot(rows_in, w_up, preferred_element_type=jnp.float32)
        sigmoid_gate = jax.nn.sigmoid(pre_gate)
        hidden = (pre_gate * sigmoid_gate * pre_up).astype(jnp.bfloat16)
        parts = jnp.einsum("rfh,fhd->frd", hidden.astype(jnp.float32).reshape(slot_rows, N_FSDP, shard),
                           w_down.astype(jnp.float32).reshape(N_FSDP, shard, D))
        expert_out = round_sum(parts)
        d_hidden = jnp.dot(grad_rows, w_down.T, preferred_element_type=jnp.float32)
        d_pre_gate = (d_hidden * pre_up * sigmoid_gate * (1.0 + pre_gate * (1.0 - sigmoid_gate))).astype(jnp.bfloat16)
        d_pre_up = (d_hidden * pre_gate * sigmoid_gate).astype(jnp.bfloat16)
        d_down = jnp.dot(hidden.T, grad_rows, preferred_element_type=jnp.float32)
        d_gate_w = jnp.dot(rows_in.T, d_pre_gate, preferred_element_type=jnp.float32)
        d_up_w = jnp.dot(rows_in.T, d_pre_up, preferred_element_type=jnp.float32)
        back_parts = jnp.einsum("rfh,dfh->frd", d_pre_gate.astype(jnp.float32).reshape(slot_rows, N_FSDP, shard),
                                w_gate.astype(jnp.float32).reshape(D, N_FSDP, shard))
        back_parts = back_parts + jnp.einsum("rfh,dfh->frd", d_pre_up.astype(jnp.float32).reshape(slot_rows, N_FSDP, shard),
                                             w_up.astype(jnp.float32).reshape(D, N_FSDP, shard))
        d_rows = round_sum(back_parts)
        return expert_out, d_rows, d_gate_w, d_up_w, d_down

    expert_out, d_rows, d_gate_weight, d_up_weight, d_down_weight = lax.map(
        one_expert, (table, gate_weight, up_weight, down_weight))
    per_pair = expert_out[flat_ids, row_pos].astype(jnp.float32).reshape(TOKENS, 2, D)
    mixed = jnp.sum(gate_probs[:, :, None] * per_pair, axis=1).astype(jnp.bfloat16)
    d_gates = jnp.sum(cotangent.astype(jnp.float32)[:, None, :] * per_pair, axis=2)
    d_tokens = jnp.sum(d_rows[flat_ids, row_pos].astype(jnp.float32).reshape(TOKENS, 2, D), axis=1).astype(jnp.bfloat16)
    return mixed, d_tokens, d_gates, d_gate_weight, d_up_weight, d_down_weight
```

```python
import jax
import jax.numpy as jnp
from jax import lax
from jax.sharding import PartitionSpec as P


def per_device(tokens, gate_probs, expert_ids, cotangent, gate_weight, up_weight, down_weight):
    tok_rows, columns = tokens.shape
    num_experts = lax.axis_size("expert")
    shard = gate_weight.shape[2]
    f32, bf16 = jnp.float32, jnp.bfloat16
    contract_rows = (((0,), (0,)), ((), ()))
    contract_cols = (((1,), (1,)), ((), ()))

    weights = jnp.concatenate([gate_weight[0].T, up_weight[0].T, down_weight[0]], axis=0)
    weights = lax.all_gather(weights, "expert", axis=0)
    onehot = (expert_ids[:, :, None] == jnp.arange(num_experts)[None, None, :]).astype(f32)
    probs = jnp.sum(gate_probs[:, :, None] * onehot, axis=1)
    toks = lax.all_gather(tokens, "fsdp", axis=0, tiled=True)
    probs = lax.all_gather(probs, "fsdp", axis=0, tiled=True)
    cots = lax.all_gather(cotangent, "fsdp", axis=0, tiled=True)

    w_gate = weights[:, :shard].reshape(-1, columns)
    w_up = weights[:, shard : 2 * shard].reshape(-1, columns)
    w_down = weights[:, 2 * shard :].reshape(-1, columns)
    rows = toks.shape[0]

    pre_gate = lax.dot_general(toks, w_gate, contract_cols, preferred_element_type=f32)
    pre_up = lax.dot_general(toks, w_up, contract_cols, preferred_element_type=f32)
    wide = jnp.broadcast_to(probs[:, :, None], (rows, num_experts, shard)).reshape(rows, -1)
    sig = jax.nn.sigmoid(pre_gate)
    hidden = pre_gate * sig * pre_up
    hidden_p = (wide * hidden).astype(bf16)
    mixed_part = jnp.dot(hidden_p, w_down, preferred_element_type=f32).astype(bf16)
    mixed = lax.psum_scatter(mixed_part, "fsdp", scatter_dimension=0, tiled=True)

    d_raw = lax.dot_general(cots, w_down, contract_cols, preferred_element_type=f32)
    gates_part = jnp.sum((hidden * d_raw).reshape(rows, num_experts, shard), axis=2)
    d_hidden = wide * d_raw
    d_pre_gate = (d_hidden * pre_up * sig * (1.0 + pre_gate * (1.0 - sig))).astype(bf16)
    d_pre_up = (d_hidden * pre_gate * sig).astype(bf16)
    back = jnp.dot(d_pre_gate, w_gate, preferred_element_type=f32)
    back = back + jnp.dot(d_pre_up, w_up, preferred_element_type=f32)
    d_tokens = lax.psum_scatter(back.astype(bf16), "fsdp", scatter_dimension=0, tiled=True)

    gates = lax.psum_scatter(gates_part, "fsdp", scatter_dimension=0, tiled=True)
    d_gates = jnp.sum(gates[:, None, :] * onehot, axis=2)

    d_gate = lax.dot_general(d_pre_gate, toks, contract_rows, preferred_element_type=f32)
    d_up = lax.dot_general(d_pre_up, toks, contract_rows, preferred_element_type=f32)
    d_down = lax.dot_general(hidden_p, cots, contract_rows, preferred_element_type=f32)
    grads = jnp.concatenate(
        [g.astype(bf16).reshape(num_experts, shard, columns) for g in (d_gate, d_up, d_down)],
        axis=1,
    )
    grads = lax.psum_scatter(grads, "expert", scatter_dimension=0, tiled=True)[0].astype(f32)
    return (
        mixed,
        d_tokens,
        d_gates,
        grads[:shard].T[None],
        grads[shard : 2 * shard].T[None],
        grads[2 * shard :][None],
    )


def solution(mesh):
    tok = P(("expert", "fsdp"), None)
    col = P("expert", None, "fsdp")
    row = P("expert", "fsdp", None)
    return jax.shard_map(
        per_device,
        mesh=mesh,
        in_specs=(tok, tok, tok, tok, col, col, row),
        out_specs=(tok, tok, tok, col, col, row),
        check_vma=False,
    )
```

```python
import jax
import jax.numpy as jnp
from jax import lax
from jax.sharding import PartitionSpec as P

F32, BF16 = jnp.float32, jnp.bfloat16
CONTRACT_ROWS = (((0,), (0,)), ((), ()))
CONTRACT_COLS = (((1,), (1,)), ((), ()))


def hop(value, axis, step):
    size = lax.axis_size(axis)
    return lax.ppermute(value, axis, [(i, i ^ step) for i in range(size)])


def inner_size(size):
    inner = 1
    while inner * inner * 4 <= size:
        inner *= 2
    return inner


def gather_shards(value, inner, outer):
    column = [value] + [hop(value, "fsdp", k * inner) for k in range(1, outer)]
    return [column] + [[hop(v, "fsdp", j) for v in column] for j in range(1, inner)]


def scatter_sum(parts, inner, outer):
    column = []
    for k in range(outer):
        total = parts[0][k]
        for j in range(1, inner):
            total = total + hop(parts[j][k].astype(BF16), "fsdp", j).astype(F32)
        column.append(total)
    total = column[0]
    for k in range(1, outer):
        total = total + hop(column[k].astype(BF16), "fsdp", k * inner).astype(F32)
    return total


def per_device(tokens, gate_probs, expert_ids, cotangent, gate_weight, up_weight, down_weight):
    tok_rows, columns = tokens.shape
    experts = lax.axis_size("expert")
    inner = inner_size(lax.axis_size("fsdp"))
    outer = lax.axis_size("fsdp") // inner
    me = lax.axis_index("expert")

    own = (gate_weight[0], up_weight[0], down_weight[0])
    weights = {0: own}
    for r in range(2, experts, 2):
        weights[r] = tuple(hop(w, "expert", r) for w in own)
    for r in range(0, experts, 2):
        weights[r + 1] = tuple(hop(w, "expert", 1) for w in weights[r])

    toks = gather_shards(tokens, inner, outer)
    route = jnp.concatenate([gate_probs.T, expert_ids.T.astype(F32)], axis=0)
    routes = gather_shards(route, inner, outer)
    cots = gather_shards(cotangent, inner, outer)

    order = list(range(experts))
    mixed_parts, back_parts, gate_parts = [], [], []
    saved = []
    for j in range(inner):
        x = jnp.concatenate(toks[j], axis=0)
        rt = jnp.concatenate(routes[j], axis=1)
        mixed = 0.0
        kept = []
        for r in order:
            w_gate, w_up, w_down = weights[r]
            e = (me ^ r).astype(F32)
            prob = jnp.sum(jnp.where(rt[2:] == e, rt[:2], 0.0), axis=0)[:, None]
            pre_gate = jnp.dot(x, w_gate, preferred_element_type=F32)
            pre_up = jnp.dot(x, w_up, preferred_element_type=F32)
            sig = jax.nn.sigmoid(pre_gate)
            silu = pre_gate * sig
            slope = pre_up * sig * (1.0 + pre_gate * (1.0 - sig))
            hidden = silu * pre_up
            hidden_p = (prob * hidden).astype(BF16)
            mixed = mixed + jnp.dot(hidden_p, w_down, preferred_element_type=F32)
            kept.append((prob, silu.astype(BF16), slope.astype(BF16), hidden.astype(BF16), hidden_p))
        mixed_parts.append(mixed.reshape(outer, tok_rows, columns))
        saved.append((x, rt, kept))
    mixed = scatter_sum(mixed_parts, inner, outer).astype(BF16)

    grads = {r: None for r in order}
    for j in range(inner):
        x, rt, kept = saved[j]
        c = jnp.concatenate(cots[j], axis=0)
        back = 0.0
        pair = jnp.zeros((2, x.shape[0]), F32)
        for r in order:
            w_gate, w_up, w_down = weights[r]
            prob, silu, slope, hidden, hidden_p = kept[r]
            e = (me ^ r).astype(F32)
            d_raw = lax.dot_general(c, w_down, CONTRACT_COLS, preferred_element_type=F32)
            inner_product = jnp.sum(hidden.astype(F32) * d_raw, axis=1)
            pair = pair + jnp.where(rt[2:] == e, inner_product[None], 0.0)
            d_hidden = prob * d_raw
            d_gate = (d_hidden * slope.astype(F32)).astype(BF16)
            d_up = (d_hidden * silu.astype(F32)).astype(BF16)
            back = back + lax.dot_general(d_gate, w_gate, CONTRACT_COLS, preferred_element_type=F32)
            back = back + lax.dot_general(d_up, w_up, CONTRACT_COLS, preferred_element_type=F32)
            grad = (
                lax.dot_general(x, d_gate, CONTRACT_ROWS, preferred_element_type=F32),
                lax.dot_general(x, d_up, CONTRACT_ROWS, preferred_element_type=F32),
                lax.dot_general(hidden_p, c, CONTRACT_ROWS, preferred_element_type=F32),
            )
            grads[r] = grad if grads[r] is None else tuple(a + b for a, b in zip(grads[r], grad))
        back_parts.append(back.reshape(outer, tok_rows, columns))
        gate_parts.append(jnp.moveaxis(pair.reshape(2, outer, tok_rows), 1, 0))
    d_tokens = scatter_sum(back_parts, inner, outer).astype(BF16)
    flat = jnp.stack([jnp.stack([g[k] for k in range(outer)]) for g in gate_parts])
    d_gates = flat[0]
    for j in range(1, inner):
        d_gates = d_gates + hop(flat[j], "fsdp", j)
    total = d_gates[0]
    for k in range(1, outer):
        total = total + hop(d_gates[k], "fsdp", k * inner)
    d_gates = total.T

    chip = {}
    for r in range(0, experts, 2):
        chip[r] = tuple(
            a + hop(b.astype(BF16), "expert", 1).astype(F32) for a, b in zip(grads[r], grads[r + 1])
        )
    final = chip[0]
    for r in range(2, experts, 2):
        final = tuple(
            a + hop(b.astype(BF16), "expert", r).astype(F32) for a, b in zip(final, chip[r])
        )
    return (mixed, d_tokens, d_gates) + tuple(g[None] for g in final)


def solution(mesh):
    tok = P(("expert", "fsdp"), None)
    col = P("expert", None, "fsdp")
    row = P("expert", "fsdp", None)
    return jax.shard_map(
        per_device,
        mesh=mesh,
        in_specs=(tok, tok, tok, tok, col, col, row),
        out_specs=(tok, tok, tok, col, col, row),
        check_vma=False,
    )
```

```python
import functools

import jax
import jax.numpy as jnp
from jax import lax
from jax.experimental import pallas as pl
from jax.experimental.pallas import tpu as pltpu
from jax.sharding import PartitionSpec as P

F32, BF16 = jnp.float32, jnp.bfloat16
CONTRACT_COLS = (((1,), (1,)), ((), ()))
ROUTE_ROWS = 8
VMEM_LIMIT = 48 * 1024 * 1024


def hop(value, axis, step):
    return lax.ppermute(value, axis, [(i, i ^ step) for i in range(lax.axis_size(axis))])


def inner_size(size):
    inner = 1
    while inner * inner * 4 <= size:
        inner *= 2
    return inner


def after(value, *earlier):
    return lax.optimization_barrier((value,) + earlier)[0]


def nt(a, b):
    return lax.dot_general(a, b, CONTRACT_COLS, preferred_element_type=F32)


def nn(a, b):
    return jnp.dot(a, b, preferred_element_type=F32)


def block_kernel(steps, shards, rows, has_acc, with_xt, me_ref, *refs):
    refs = list(refs)
    pays = [refs.pop(0) for _ in range(shards)]
    weights = [(refs.pop(0), refs.pop(0)) for _ in steps]
    accs = [refs.pop(0) for _ in range(shards)] if has_acc else None
    outs = [refs.pop(0) for _ in range(shards)]
    dg_ref, du_ref, hpt_ref = refs.pop(0), refs.pop(0), refs.pop(0)
    xt_ref = refs.pop(0) if with_xt else None
    x_ref, c_ref, mixed_ref, back_ref = refs
    total = shards * rows
    columns = x_ref.shape[1]
    for j, pay in enumerate(pays):
        x_ref[j * rows : (j + 1) * rows, :] = pay[0:rows, :]
        c_ref[j * rows : (j + 1) * rows, :] = pay[rows : 2 * rows, :]
    eye = (
        lax.broadcasted_iota(jnp.int32, (rows, rows), 0)
        == lax.broadcasted_iota(jnp.int32, (rows, rows), 1)
    ).astype(BF16)
    routes = [pay[2 * rows : 2 * rows + ROUTE_ROWS, 0:rows] for pay in pays]
    stand = jnp.concatenate([nt(eye, route) for route in routes], axis=0)
    lying = jnp.concatenate([route.astype(F32) for route in routes], axis=1)
    gates = [jnp.zeros((1, total), F32), jnp.zeros((1, total), F32)]
    for i, (step, (gu, down)) in enumerate(zip(steps, weights)):
        e = (me_ref[0] ^ step).astype(F32)
        prob = jnp.where(stand[:, 4:5] == e, stand[:, 0:1] + stand[:, 2:3], 0.0)
        prob = prob + jnp.where(stand[:, 5:6] == e, stand[:, 1:2] + stand[:, 3:4], 0.0)
        pre_gate = nn(x_ref[...], gu[0])
        pre_up = nn(x_ref[...], gu[1])
        d_raw = nt(c_ref[...], down[...])
        sig = jax.nn.sigmoid(pre_gate)
        silu = pre_gate * sig
        hidden = silu * pre_up
        hidden_p = (prob * hidden).astype(BF16)
        product = (hidden * d_raw).astype(BF16)
        sums = nt(jnp.ones((8, product.shape[1]), BF16), product)[0:1]
        for k in range(2):
            gates[k] = gates[k] + jnp.where(lying[4 + k : 5 + k] == e, sums, 0.0)
        d_hidden = prob * d_raw
        d_gate = (d_hidden * pre_up * sig * (1.0 + pre_gate * (1.0 - sig))).astype(BF16)
        d_up = (d_hidden * silu).astype(BF16)
        dg_ref[i] = d_gate
        du_ref[i] = d_up
        hpt_ref[i] = hidden_p.T
        mixed = nn(hidden_p, down[...])
        back = nt(d_gate, gu[0]) + nt(d_up, gu[1])
        if i == 0:
            mixed_ref[...] = mixed
            back_ref[...] = back
        else:
            mixed_ref[...] += mixed
            back_ref[...] += back
    if with_xt:
        xt_ref[...] = x_ref[...].T
    for j, out in enumerate(outs):
        at = slice(j * rows, (j + 1) * rows)
        mixed, back = mixed_ref[at, :], back_ref[at, :]
        pair = jnp.concatenate([g[:, at] for g in gates] + [jnp.zeros((ROUTE_ROWS - 2, rows), F32)], axis=0)
        pair = jnp.concatenate([pair, jnp.zeros((ROUTE_ROWS, columns - rows), F32)], axis=1)
        if has_acc:
            mixed = mixed + accs[j][0:rows, :]
            back = back + accs[j][rows : 2 * rows, :]
            pair = pair + accs[j][2 * rows :, :]
        out[0:rows, :] = mixed.astype(out.dtype)
        out[rows : 2 * rows, :] = back.astype(out.dtype)
        out[2 * rows :, :] = pair.astype(out.dtype)


def block(me, steps, pays, weights, accs, rows, send_dtype, with_xt):
    shards, experts = len(pays), len(steps)
    columns = pays[0].shape[1]
    width = weights[0][1].shape[0]
    total = shards * rows
    args = list(pays) + [w for pair in weights for w in pair] + list(accs or [])
    outs = [jax.ShapeDtypeStruct(pays[0].shape, F32 if j == 0 else send_dtype) for j in range(shards)]
    outs += [jax.ShapeDtypeStruct((experts, total, width), BF16)] * 2
    outs += [jax.ShapeDtypeStruct((experts, width, total), BF16)]
    if with_xt:
        outs += [jax.ShapeDtypeStruct((columns, total), BF16)]
    vmem = pl.BlockSpec(memory_space=pltpu.VMEM)
    moved = sum(a.size * a.dtype.itemsize for a in args + outs)
    res = pl.pallas_call(
        functools.partial(block_kernel, tuple(steps), shards, rows, accs is not None, with_xt),
        out_shape=outs,
        in_specs=[pl.BlockSpec(memory_space=pltpu.SMEM)] + [vmem] * len(args),
        out_specs=[vmem] * len(outs),
        scratch_shapes=[pltpu.VMEM((total, columns), BF16)] * 2 + [pltpu.VMEM((total, columns), F32)] * 2,
        compiler_params=pltpu.CompilerParams(vmem_limit_bytes=VMEM_LIMIT),
        cost_estimate=pl.CostEstimate(
            flops=12 * total * columns * width * experts,
            bytes_accessed=moved,
            transcendentals=total * width * experts,
        ),
        name="block",
    )(me, *args)
    return res[:shards], res[shards : shards + 3], (res[-1] if with_xt else None)


def grad_kernel(blocks, shards, rows, slots, *refs):
    refs = list(refs)
    pays = [[refs.pop(0) for _ in range(shards)] for _ in range(blocks)]
    xts = [refs.pop(0) for _ in range(blocks)]
    acts = [(refs.pop(0), refs.pop(0), refs.pop(0)) for _ in range(blocks)]
    gu_out, down_out, c_ref = refs
    total = shards * rows
    for b in range(blocks):
        for j in range(shards):
            at = b * total + j * rows
            c_ref[at : at + rows, :] = pays[b][j][rows : 2 * rows, :]
    height = gu_out.shape[1]
    part = height // 2
    for h in range(0, height, part):
        gate = nn(xts[0][h : h + part, :], acts[0][0][slots[0]])
        up = nn(xts[0][h : h + part, :], acts[0][1][slots[0]])
        for b in range(1, blocks):
            gate = gate + nn(xts[b][h : h + part, :], acts[b][0][slots[b]])
            up = up + nn(xts[b][h : h + part, :], acts[b][1][slots[b]])
        gu_out[0, h : h + part, :] = gate.astype(gu_out.dtype)
        gu_out[1, h : h + part, :] = up.astype(gu_out.dtype)
    down = nn(acts[0][2][slots[0]], c_ref[0:total, :])
    for b in range(1, blocks):
        down = down + nn(acts[b][2][slots[b]], c_ref[b * total : (b + 1) * total, :])
    down_out[...] = down.astype(down_out.dtype)


def grad(pays, xts, acts, slots, rows, dtype):
    blocks, shards = len(pays), len(pays[0])
    columns = pays[0][0].shape[1]
    width = acts[0][0].shape[2]
    tokens = blocks * shards * rows
    args = [p for ps in pays for p in ps] + list(xts) + [a for act in acts for a in act]
    outs = [
        jax.ShapeDtypeStruct((2, columns, width), dtype),
        jax.ShapeDtypeStruct((width, columns), dtype),
    ]
    vmem = pl.BlockSpec(memory_space=pltpu.VMEM)
    return pl.pallas_call(
        functools.partial(grad_kernel, blocks, shards, rows, tuple(slots)),
        out_shape=outs,
        in_specs=[vmem] * len(args),
        out_specs=[vmem] * 2,
        scratch_shapes=[pltpu.VMEM((tokens, columns), BF16)],
        compiler_params=pltpu.CompilerParams(vmem_limit_bytes=VMEM_LIMIT),
        cost_estimate=pl.CostEstimate(
            flops=6 * tokens * columns * width,
            bytes_accessed=sum(a.size * a.dtype.itemsize for a in args + outs),
            transcendentals=0,
        ),
        name="grad",
    )(*args)


def per_device(tokens, gate_probs, expert_ids, cotangent, gate_weight, up_weight, down_weight):
    rows, columns = tokens.shape
    experts = lax.axis_size("expert")
    inner = inner_size(lax.axis_size("fsdp"))
    outer = lax.axis_size("fsdp") // inner
    me = lax.axis_index("expert").astype(jnp.int32).reshape(1)

    high = lax.reduce_precision(gate_probs, 8, 7)
    route = jnp.concatenate([high, gate_probs - high, expert_ids.astype(F32)], axis=1).T
    route = jnp.pad(route, ((0, ROUTE_ROWS - route.shape[0]), (0, columns - rows))).astype(BF16)
    own_pay = jnp.concatenate([tokens, cotangent, route], axis=0)

    own = (jnp.stack([gate_weight[0], up_weight[0]]), down_weight[0])
    weights = {0: own}
    for r in range(2, experts, 2):
        weights[r] = tuple(hop(w, "expert", r) for w in own)
    for r in range(0, experts, 2):
        weights[r + 1] = tuple(hop(w, "expert", 1) for w in weights[r])

    column = {0: own_pay}
    bit = outer // 2
    last = None
    while bit >= 1:
        for k in sorted(column):
            source = column[k] if last is None else after(column[k], last)
            column[k | bit] = last = hop(source, "fsdp", bit * inner)
        bit //= 2
    pays = {k: [v] + [hop(v, "fsdp", j) for j in range(1, inner)] for k, v in column.items()}

    near, far = [0, 1], list(range(2, experts))
    acts, xts, parts = {}, {}, {}
    arrival = list(column)
    early, late = arrival[:-1], arrival[-1:]
    for k in early:
        parts[k], act, xts[k] = block(
            me, near, pays[k], [weights[r] for r in near], None, rows, F32, True
        )
        acts[k] = [(act, near)]
    for k in late:
        parts[k], act, xts[k] = block(
            me, near + far, pays[k], [weights[r] for r in near + far], None, rows, BF16, True
        )
        acts[k] = [(act, near + far)]
    for k in early:
        parts[k], act, _ = block(
            me, far, pays[k], [weights[r] for r in far], parts[k], rows, BF16, False
        )
        acts[k].append((act, far))

    sums = {}
    for k in range(outer):
        sums[k] = parts[k][0]
        for j in range(1, inner):
            sums[k] = sums[k] + hop(parts[k][j], "fsdp", j).astype(F32)
    bit = 1
    while bit < outer:
        for k in reversed(range(bit, outer, 2 * bit)):
            sums[k - bit] = sums[k - bit] + hop(sums[k].astype(BF16), "fsdp", bit * inner).astype(F32)
        bit *= 2
    mixed = sums[0][:rows].astype(BF16)
    d_tokens = sums[0][rows : 2 * rows].astype(BF16)
    d_gates = sums[0][2 * rows : 2 * rows + 2, :rows].T

    order = range(outer)
    grads = {}
    for r in far[::-1] + near[::-1]:
        chosen, slots = [], []
        for k in order:
            for act, names in acts[k]:
                if r in names:
                    chosen.append(act)
                    slots.append(names.index(r))
        grads[r] = grad(
            [pays[k] for k in order], [xts[k] for k in order], chosen, slots, rows,
            BF16 if r % 2 else F32,
        )
    chip = {}
    for r in range(0, experts, 2):
        chip[r] = [a + hop(b, "expert", 1).astype(F32) for a, b in zip(grads[r], grads[r + 1])]
    final = chip[0]
    for r in range(2, experts, 2):
        final = [a + hop(b.astype(BF16), "expert", r).astype(F32) for a, b in zip(final, chip[r])]
    gu, down = final
    return mixed, d_tokens, d_gates, gu[0][None], gu[1][None], down[None]


def solution(mesh):
    tok = P(("expert", "fsdp"), None)
    col = P("expert", None, "fsdp")
    row = P("expert", "fsdp", None)
    return jax.shard_map(
        per_device,
        mesh=mesh,
        in_specs=(tok, tok, tok, tok, col, col, row),
        out_specs=(tok, tok, tok, col, col, row),
        check_vma=False,
    )
```

```python
import functools

import jax
import jax.numpy as jnp
from jax import lax
from jax.experimental import pallas as pl
from jax.experimental.pallas import tpu as pltpu
from jax.sharding import PartitionSpec as P

F32, BF16 = jnp.float32, jnp.bfloat16
CONTRACT_COLS = (((1,), (1,)), ((), ()))
ROUTE_ROWS = 8
VMEM_LIMIT = 24 * 1024 * 1024
ANY = pl.BlockSpec(memory_space=pl.ANY)
VMEM = pl.BlockSpec(memory_space=pltpu.VMEM)


def hop(value, axis, step):
    return lax.ppermute(value, axis, [(i, i ^ step) for i in range(lax.axis_size(axis))])


def line_hop(value, inner, pairs):
    return lax.ppermute(
        value, "fsdp", [(a * inner + y, b * inner + y) for a, b in pairs for y in range(inner)]
    )


def inner_size(size):
    inner = 1
    while inner * inner * 4 <= size:
        inner *= 2
    return inner


def after(value, *earlier):
    return lax.optimization_barrier((value,) + earlier)[0]


def nt(a, b):
    return lax.dot_general(a, b, CONTRACT_COLS, preferred_element_type=F32)


def nn(a, b):
    return jnp.dot(a, b, preferred_element_type=F32)


def block_kernel(steps, shards, rows, at, has_acc, with_t, aliased, me_ref, *refs):
    refs = list(refs)
    take = lambda n: [refs.pop(0) for _ in range(n)]
    pays, weights = take(shards), take(len(steps))
    accs = take(shards) if has_acc else []
    take(aliased)
    outs = take(shards)
    (act_all,) = take(1)
    t_all = take(2) if with_t else []
    x_ref, c_ref, mixed_ref, back_ref, w_ref, act_ref = take(6)
    t_refs = take(2) if with_t else []
    acc_refs = take(shards) if has_acc else []
    w_sem, act_sem, t_sem, acc_sem = take(4)
    total = shards * rows
    columns = x_ref.shape[1]
    w_copies = [
        [pltpu.make_async_copy(w.at[m], w_ref.at[i, m], w_sem.at[i, m]) for m in range(3)]
        for i, w in enumerate(weights)
    ]
    for group in w_copies:
        for m in (0, 1, 2):
            group[m].start()
    acc_copies = [
        pltpu.make_async_copy(a, r, acc_sem.at[j]) for j, (a, r) in enumerate(zip(accs, acc_refs))
    ]
    for copy in acc_copies:
        copy.start()
    for j, pay in enumerate(pays):
        x_ref[j * rows : (j + 1) * rows, :] = pay[0:rows, :]
        c_ref[j * rows : (j + 1) * rows, :] = pay[rows : 2 * rows, :]
    t_copies = []
    if with_t:
        for n, source in enumerate((x_ref, c_ref)):
            t_refs[n][...] = source[...].T
            t_copies.append(
                pltpu.make_async_copy(
                    t_refs[n], t_all[n].at[:, at * total : (at + 1) * total], t_sem.at[n]
                )
            )
            t_copies[n].start()
    eye = (
        lax.broadcasted_iota(jnp.int32, (rows, rows), 0)
        == lax.broadcasted_iota(jnp.int32, (rows, rows), 1)
    ).astype(BF16)
    routes = [pay[2 * rows : 2 * rows + ROUTE_ROWS, 0:rows] for pay in pays]
    stand = jnp.concatenate([nt(eye, route) for route in routes], axis=0)
    lying = jnp.concatenate([route.astype(F32) for route in routes], axis=1)
    gates = [jnp.zeros((1, total), F32), jnp.zeros((1, total), F32)]
    act_copies = []
    for i, step in enumerate(steps):
        e = (me_ref[0] ^ step).astype(F32)
        prob = jnp.where(stand[:, 4:5] == e, stand[:, 0:1] + stand[:, 2:3], 0.0)
        prob = prob + jnp.where(stand[:, 5:6] == e, stand[:, 1:2] + stand[:, 3:4], 0.0)
        w_copies[i][0].wait()
        pre_gate = nn(x_ref[...], w_ref[i, 0])
        w_copies[i][1].wait()
        pre_up = nn(x_ref[...], w_ref[i, 1])
        w_copies[i][2].wait()
        d_raw = nn(c_ref[...], w_ref[i, 2])
        sig = jax.nn.sigmoid(pre_gate)
        silu = pre_gate * sig
        hidden = silu * pre_up
        hidden_p = (prob * hidden).astype(BF16)
        product = (hidden * d_raw).astype(BF16)
        sums = nt(jnp.ones((8, product.shape[1]), BF16), product)[0:1]
        for k in range(2):
            gates[k] = gates[k] + jnp.where(lying[4 + k : 5 + k] == e, sums, 0.0)
        d_hidden = prob * d_raw
        d_gate = (d_hidden * pre_up * sig * (1.0 + pre_gate * (1.0 - sig))).astype(BF16)
        d_up = (d_hidden * silu).astype(BF16)
        for m, value in enumerate((d_gate, d_up, hidden_p)):
            act_ref[i, m] = value
            copy = pltpu.make_async_copy(
                act_ref.at[i, m],
                act_all.at[step, m, at * total : (at + 1) * total, :],
                act_sem.at[i, m],
            )
            copy.start()
            act_copies.append(copy)
        mixed = nt(hidden_p, w_ref[i, 2])
        back = nt(d_gate, w_ref[i, 0]) + nt(d_up, w_ref[i, 1])
        if i == 0:
            mixed_ref[...] = mixed
            back_ref[...] = back
        else:
            mixed_ref[...] += mixed
            back_ref[...] += back
    for copy in acc_copies:
        copy.wait()
    for j, out in enumerate(outs):
        part = slice(j * rows, (j + 1) * rows)
        mixed, back = mixed_ref[part, :], back_ref[part, :]
        pair = jnp.concatenate(
            [g[:, part] for g in gates] + [jnp.zeros((ROUTE_ROWS - 2, rows), F32)], axis=0
        )
        pair = jnp.concatenate([pair, jnp.zeros((ROUTE_ROWS, columns - rows), F32)], axis=1)
        if has_acc:
            mixed = mixed + acc_refs[j][0:rows, :]
            back = back + acc_refs[j][rows : 2 * rows, :]
            pair = pair + acc_refs[j][2 * rows :, :]
        out[0:rows, :] = mixed.astype(out.dtype)
        out[rows : 2 * rows, :] = back.astype(out.dtype)
        out[2 * rows :, :] = pair.astype(out.dtype)
    for copy in t_copies + act_copies:
        copy.wait()


def block(me, steps, pays, weights, accs, shared, at, rows, send_dtype, with_t, experts, blocks):
    shards, count = len(pays), len(steps)
    columns = pays[0].shape[1]
    width = weights[0].shape[2]
    total = shards * rows
    outs = [
        jax.ShapeDtypeStruct(pays[0].shape, F32 if j == 0 else send_dtype) for j in range(shards)
    ]
    filled = [jax.ShapeDtypeStruct((experts, 3, blocks * total, width), BF16)]
    if with_t:
        filled += [jax.ShapeDtypeStruct((columns, blocks * total), BF16)] * 2
    old = list(shared[: len(filled)]) if shared else []
    args = list(pays) + list(weights) + list(accs or []) + old
    first = 1 + len(args) - len(old)
    moved = sum(a.size * a.dtype.itemsize for a in list(pays) + list(weights) + outs)
    scratch = [pltpu.VMEM((total, columns), BF16)] * 2 + [pltpu.VMEM((total, columns), F32)] * 2
    scratch += [pltpu.VMEM((count, 3, columns, width), BF16), pltpu.VMEM((count, 3, total, width), BF16)]
    if with_t:
        scratch += [pltpu.VMEM((columns, total), BF16)] * 2
    if accs:
        scratch += [pltpu.VMEM(a.shape, F32) for a in accs]
    dma = pltpu.SemaphoreType.DMA
    scratch += [dma((count, 3)), dma((count, 3)), dma((2,)), dma((shards,))]
    res = pl.pallas_call(
        functools.partial(
            block_kernel, tuple(steps), shards, rows, at, bool(accs), with_t, len(old)
        ),
        out_shape=outs + filled,
        in_specs=[pl.BlockSpec(memory_space=pltpu.SMEM)]
        + [VMEM] * shards
        + [ANY] * (len(args) - shards),
        out_specs=[VMEM] * shards + [ANY] * len(filled),
        scratch_shapes=scratch,
        input_output_aliases={first + n: shards + n for n in range(len(old))},
        compiler_params=pltpu.CompilerParams(vmem_limit_bytes=68 * total * columns),
        cost_estimate=pl.CostEstimate(
            flops=12 * total * columns * width * count,
            bytes_accessed=moved,
            transcendentals=total * width * count,
        ),
        name="block",
    )(me, *args)
    new = list(res[shards:])
    return res[:shards], new + list(shared[len(new) :] if shared else [])


def grad_kernel(count, me_ref, xt_ref, ct_ref, *refs):
    acts, outs = refs[:count], refs[count:]
    for act, out in zip(acts, outs):
        for m, left in enumerate((xt_ref, xt_ref, ct_ref)):
            out[m] = nn(left[...], act[0, m]).astype(out.dtype)


def grad(me, experts, act_all, xt_all, ct_all, dtypes):
    columns, tokens = xt_all.shape
    width = act_all.shape[3]
    part = columns // 3
    left = pl.BlockSpec((part, tokens), lambda i: (i, 0))
    chosen = [
        pl.BlockSpec((1, 3, tokens, width), functools.partial(lambda r, i: (r, 0, 0, 0), r))
        for r in experts
    ]
    return pl.pallas_call(
        functools.partial(grad_kernel, len(experts)),
        grid=(3,),
        out_shape=[jax.ShapeDtypeStruct((3, columns, width), d) for d in dtypes],
        in_specs=[pl.BlockSpec(memory_space=pltpu.SMEM), left, left] + chosen,
        out_specs=[pl.BlockSpec((3, part, width), lambda i: (0, i, 0))] * len(experts),
        compiler_params=pltpu.CompilerParams(vmem_limit_bytes=VMEM_LIMIT),
        cost_estimate=pl.CostEstimate(
            flops=6 * tokens * columns * width * len(experts),
            bytes_accessed=4 * tokens * columns,
            transcendentals=0,
        ),
        name="grad",
    )(me, xt_all, ct_all, *[act_all] * len(experts))


def final_kernel(*refs):
    parts, (gate, up, down) = refs[:-3], refs[-3:]
    for m, out in enumerate((gate, up, down)):
        value = parts[0][m].astype(F32)
        for part in parts[1:]:
            value = value + part[m].astype(F32)
        out[0] = value.T if m == 2 else value


def final_sum(parts):
    _, columns, width = parts[0].shape
    part = columns // 3
    tall = jax.ShapeDtypeStruct((1, columns, width), F32)
    return pl.pallas_call(
        final_kernel,
        grid=(3,),
        out_shape=[tall, tall, jax.ShapeDtypeStruct((1, width, columns), F32)],
        in_specs=[pl.BlockSpec((3, part, width), lambda i: (0, i, 0))] * len(parts),
        out_specs=[pl.BlockSpec((1, part, width), lambda i: (0, i, 0))] * 2
        + [pl.BlockSpec((1, width, part), lambda i: (0, 0, i))],
        compiler_params=pltpu.CompilerParams(vmem_limit_bytes=VMEM_LIMIT),
        name="final",
    )(*parts)


def per_device(tokens, gate_probs, expert_ids, cotangent, gate_weight, up_weight, down_weight):
    rows, columns = tokens.shape
    experts = lax.axis_size("expert")
    inner = inner_size(lax.axis_size("fsdp"))
    outer = lax.axis_size("fsdp") // inner
    me = lax.axis_index("expert").astype(jnp.int32).reshape(1)
    place = lax.axis_index("fsdp") // inner

    high = lax.reduce_precision(gate_probs, 8, 7)
    route = jnp.concatenate([high, gate_probs - high, expert_ids.astype(F32)], axis=1).T
    route = jnp.pad(route, ((0, ROUTE_ROWS - route.shape[0]), (0, columns - rows))).astype(BF16)
    own_pay = jnp.concatenate([tokens, cotangent, route], axis=0)

    groups = range(0, outer, 4)
    across = [(g + a, g + b) for g in groups for a, b in ((1, 2), (2, 1))]
    outward = [(g + a, g + b) for g in groups for a, b in ((1, 0), (2, 3))]
    inward = [(b, a) for a, b in outward]
    beside = lambda v: [hop(v, "fsdp", j) for j in range(1, inner)]
    middle = ((place + 1) & 2) != 0

    own_w = jnp.stack([gate_weight[0], up_weight[0], down_weight[0].T])
    column = {0: own_pay}
    column[1] = hop(own_pay, "fsdp", inner)
    cross1 = line_hop(own_pay, inner, across)
    pays = {0: [own_pay] + beside(own_pay)}
    weights = {0: own_w, 1: hop(own_w, "expert", 1)}
    for r in range(2, experts, 2):
        weights[r] = hop(own_w, "expert", r)
        weights[r + 1] = hop(weights[r], "expert", 1)
    pays[1] = [column[1]] + beside(column[1])
    cross2 = line_hop(column[1], inner, across)
    column[2] = jnp.where(middle, cross2, line_hop(cross1, inner, outward))
    pays[2] = [column[2]] + beside(column[2])
    column[3] = jnp.where(middle, cross1, line_hop(cross2, inner, outward))
    pays[3] = [column[3]] + beside(column[3])

    near, far = [0, 1], list(range(2, experts))
    near_w, far_w = [weights[r] for r in near], [weights[r] for r in far]
    size = dict(experts=experts, blocks=4)
    keep, shared = {}, None
    tick = me
    keep[0], shared = block(tick, near, pays[0], near_w, None, shared, 0, rows, F32, True, **size)
    tick = after(me, shared[0], column[2])
    keep[1], shared = block(tick, near, pays[1], near_w, None, shared, 1, rows, F32, True, **size)
    tick = after(me, shared[0], column[3])
    keep[2], shared = block(tick, near, pays[2], near_w, None, shared, 2, rows, F32, True, **size)
    done = {}
    tick = after(me, shared[0])
    done[0], shared = block(tick, far, pays[0], far_w, keep[0], shared, 0, rows, BF16, False, **size)
    tick = after(me, shared[0])
    done[3], shared = block(
        tick, near + far, pays[3], near_w + far_w, None, shared, 3, rows, BF16, True, **size
    )
    tick = after(me, shared[0])
    done[2], shared = block(tick, far, pays[2], far_w, keep[2], shared, 2, rows, BF16, False, **size)
    tick = after(me, shared[0])
    done[1], shared = block(tick, far, pays[1], far_w, keep[1], shared, 1, rows, BF16, False, **size)
    act_all, xt_all, ct_all = shared

    def join(k, sends):
        total = done[k][0]
        for j in range(1, inner):
            total = total + hop(sends[j - 1], "fsdp", j).astype(F32)
        return total

    small = lambda v: v.astype(BF16)
    sum3 = join(3, done[3][1:])
    sum2 = join(2, done[2][1:])
    sum1 = join(1, [after(s, sum3) for s in done[1][1:]])
    sum0 = join(0, [after(s, sum2) for s in done[0][1:]])
    up3 = line_hop(small(sum3), inner, inward)
    up2 = line_hop(small(sum2), inner, inward)
    sum2 = sum2 + up3.astype(F32)
    sum3 = sum3 + up2.astype(F32)
    sum1 = sum1 + line_hop(small(sum2), inner, across).astype(F32)
    sum0 = sum0 + line_hop(small(sum3), inner, across).astype(F32)
    sum0 = sum0 + hop(small(sum1), "fsdp", inner).astype(F32)
    mixed, d_tokens = small(sum0[:rows]), small(sum0[rows : 2 * rows])
    d_gates = sum0[2 * rows : 2 * rows + 2, :rows].T

    tick = after(me, act_all)
    order = far[::-1]
    far_grads = dict(zip(order, grad(tick, order, act_all, xt_all, ct_all, [BF16] * len(order))))
    arrived = []
    for r in range(2, experts, 2):
        chip = far_grads[r].astype(F32) + hop(far_grads[r + 1], "expert", 1).astype(F32)
        chip = small(chip)
        tick = after(me, chip)
        arrived.append(hop(chip, "expert", r))
    near_grads = grad(tick, near[::-1], act_all, xt_all, ct_all, [BF16, F32])
    chip = near_grads[1] + hop(near_grads[0], "expert", 1).astype(F32)
    gate, up, down = final_sum([chip] + arrived)
    return mixed, d_tokens, d_gates, gate, up, down


def solution(mesh):
    tok = P(("expert", "fsdp"), None)
    col = P("expert", None, "fsdp")
    row = P("expert", "fsdp", None)
    return jax.shard_map(
        per_device,
        mesh=mesh,
        in_specs=(tok, tok, tok, tok, col, col, row),
        out_specs=(tok, tok, tok, col, col, row),
        check_vma=False,
    )
```

```python
import functools

import jax
import jax.numpy as jnp
from jax import lax
from jax.experimental import pallas as pl
from jax.experimental.pallas import tpu as pltpu
from jax.sharding import PartitionSpec as P

F32, BF16 = jnp.float32, jnp.bfloat16
CONTRACT_COLS = (((1,), (1,)), ((), ()))
ROUTE_ROWS = 8
VMEM_LIMIT = 56 * 1024 * 1024
SMALL_COST = pl.CostEstimate(flops=1000, bytes_accessed=1000, transcendentals=0)
ANY = pl.BlockSpec(memory_space=pl.ANY)
VMEM = pl.BlockSpec(memory_space=pltpu.VMEM)


def hop(value, axis, step):
    return lax.ppermute(value, axis, [(i, i ^ step) for i in range(lax.axis_size(axis))])


def line_hop(value, inner, pairs):
    return lax.ppermute(
        value, "fsdp", [(a * inner + y, b * inner + y) for a, b in pairs for y in range(inner)]
    )


def inner_size(size):
    inner = 1
    while inner * inner * 4 <= size:
        inner *= 2
    return inner


def after(value, *earlier):
    return lax.optimization_barrier((value,) + earlier)[0]


def nt(a, b):
    return lax.dot_general(a, b, CONTRACT_COLS, preferred_element_type=F32)


def nn(a, b):
    return jnp.dot(a, b, preferred_element_type=F32)


def block_kernel(steps, shards, rows, at, has_acc, with_t, aliased, me_ref, *refs):
    refs = list(refs)
    take = lambda n: [refs.pop(0) for _ in range(n)]
    pays, weights = take(shards), take(len(steps))
    accs = take(shards) if has_acc else []
    take(aliased)
    outs = take(shards)
    (act_all,) = take(1)
    t_all = take(2) if with_t else []
    x_ref, c_ref, mixed_ref, back_ref, w_ref, act_ref = take(6)
    t_refs = take(2) if with_t else []
    acc_refs = take(shards) if has_acc else []
    w_sem, act_sem, t_sem, acc_sem = take(4)
    total = shards * rows
    columns = x_ref.shape[1]
    w_copies = [
        [pltpu.make_async_copy(w.at[m], w_ref.at[i, m], w_sem.at[i, m]) for m in range(3)]
        for i, w in enumerate(weights)
    ]
    for group in w_copies:
        for m in (0, 1, 2):
            group[m].start()
    acc_copies = [
        pltpu.make_async_copy(a, r, acc_sem.at[j]) for j, (a, r) in enumerate(zip(accs, acc_refs))
    ]
    for copy in acc_copies:
        copy.start()
    for j, pay in enumerate(pays):
        x_ref[j * rows : (j + 1) * rows, :] = pay[0:rows, :]
        c_ref[j * rows : (j + 1) * rows, :] = pay[rows : 2 * rows, :]
    t_copies = []
    if with_t:
        for n, source in enumerate((x_ref, c_ref)):
            t_refs[n][...] = source[...].T
            t_copies.append(
                pltpu.make_async_copy(
                    t_refs[n], t_all[n].at[:, at * total : (at + 1) * total], t_sem.at[n]
                )
            )
            t_copies[n].start()
    eye = (
        lax.broadcasted_iota(jnp.int32, (rows, rows), 0)
        == lax.broadcasted_iota(jnp.int32, (rows, rows), 1)
    ).astype(BF16)
    routes = [pay[2 * rows : 2 * rows + ROUTE_ROWS, 0:rows] for pay in pays]
    stand = jnp.concatenate([nt(eye, route) for route in routes], axis=0)
    lying = jnp.concatenate([route.astype(F32) for route in routes], axis=1)
    gates = [jnp.zeros((1, total), F32), jnp.zeros((1, total), F32)]
    act_copies = []
    for i, step in enumerate(steps):
        e = (me_ref[0] ^ step).astype(F32)
        prob = jnp.where(stand[:, 4:5] == e, stand[:, 0:1] + stand[:, 2:3], 0.0)
        prob = prob + jnp.where(stand[:, 5:6] == e, stand[:, 1:2] + stand[:, 3:4], 0.0)
        w_copies[i][0].wait()
        pre_gate = nn(x_ref[...], w_ref[i, 0])
        w_copies[i][1].wait()
        pre_up = nn(x_ref[...], w_ref[i, 1])
        w_copies[i][2].wait()
        d_raw = nn(c_ref[...], w_ref[i, 2])
        sig = jax.nn.sigmoid(pre_gate)
        silu = pre_gate * sig
        hidden = silu * pre_up
        hidden_p = (prob * hidden).astype(BF16)
        product = (hidden * d_raw).astype(BF16)
        sums = nt(jnp.ones((8, product.shape[1]), BF16), product)[0:1]
        for k in range(2):
            gates[k] = gates[k] + jnp.where(lying[4 + k : 5 + k] == e, sums, 0.0)
        d_hidden = prob * d_raw
        d_gate = (d_hidden * pre_up * sig * (1.0 + pre_gate * (1.0 - sig))).astype(BF16)
        d_up = (d_hidden * silu).astype(BF16)
        for m, value in enumerate((d_gate, d_up, hidden_p)):
            act_ref[i, m] = value
            copy = pltpu.make_async_copy(
                act_ref.at[i, m],
                act_all.at[step, m, at * total : (at + 1) * total, :],
                act_sem.at[i, m],
            )
            copy.start()
            act_copies.append(copy)
        mixed = nt(hidden_p, w_ref[i, 2])
        back = nt(d_gate, w_ref[i, 0]) + nt(d_up, w_ref[i, 1])
        if i == 0:
            mixed_ref[...] = mixed
            back_ref[...] = back
        else:
            mixed_ref[...] += mixed
            back_ref[...] += back
    for copy in acc_copies:
        copy.wait()
    for j, out in enumerate(outs):
        part = slice(j * rows, (j + 1) * rows)
        mixed, back = mixed_ref[part, :], back_ref[part, :]
        pair = jnp.concatenate(
            [g[:, part] for g in gates] + [jnp.zeros((ROUTE_ROWS - 2, rows), F32)], axis=0
        )
        pair = jnp.concatenate([pair, jnp.zeros((ROUTE_ROWS, columns - rows), F32)], axis=1)
        if has_acc:
            mixed = mixed + acc_refs[j][0:rows, :]
            back = back + acc_refs[j][rows : 2 * rows, :]
            pair = pair + acc_refs[j][2 * rows :, :]
        out[0:rows, :] = mixed.astype(out.dtype)
        out[rows : 2 * rows, :] = back.astype(out.dtype)
        out[2 * rows :, :] = pair.astype(out.dtype)
    for copy in t_copies + act_copies:
        copy.wait()


def block(me, steps, pays, weights, accs, shared, at, *, rows, send_dtype, with_t, experts, blocks):
    shards, count = len(pays), len(steps)
    columns = pays[0].shape[1]
    width = weights[0].shape[2]
    total = shards * rows
    outs = [
        jax.ShapeDtypeStruct(pays[0].shape, F32 if j == 0 else send_dtype) for j in range(shards)
    ]
    filled = [jax.ShapeDtypeStruct((experts, 3, blocks * total, width), BF16)]
    if with_t:
        filled += [jax.ShapeDtypeStruct((columns, blocks * total), BF16)] * 2
    old = list(shared[: len(filled)]) if shared else []
    args = list(pays) + list(weights) + list(accs or []) + old
    first = 1 + len(args) - len(old)
    scratch = [pltpu.VMEM((total, columns), BF16)] * 2 + [pltpu.VMEM((total, columns), F32)] * 2
    scratch += [pltpu.VMEM((count, 3, columns, width), BF16), pltpu.VMEM((count, 3, total, width), BF16)]
    if with_t:
        scratch += [pltpu.VMEM((columns, total), BF16)] * 2
    if accs:
        scratch += [pltpu.VMEM(a.shape, F32) for a in accs]
    dma = pltpu.SemaphoreType.DMA
    scratch += [dma((count, 3)), dma((count, 3)), dma((2,)), dma((shards,))]
    res = pl.pallas_call(
        functools.partial(
            block_kernel, tuple(steps), shards, rows, at, bool(accs), with_t, len(old)
        ),
        out_shape=outs + filled,
        in_specs=[pl.BlockSpec(memory_space=pltpu.SMEM)]
        + [VMEM] * shards
        + [ANY] * (len(args) - shards),
        out_specs=[VMEM] * shards + [ANY] * len(filled),
        scratch_shapes=scratch,
        input_output_aliases={first + n: shards + n for n in range(len(old))},
        compiler_params=pltpu.CompilerParams(vmem_limit_bytes=VMEM_LIMIT),
        cost_estimate=SMALL_COST,
        name="block",
    )(me, *args)
    new = list(res[shards:])
    return res[:shards], new + list(shared[len(new) :] if shared else [])


def grad_kernel(count, me_ref, xt_ref, ct_ref, *refs):
    acts, outs = refs[:count], refs[count:]
    for act, out in zip(acts, outs):
        for m, left in enumerate((xt_ref, xt_ref, ct_ref)):
            out[m] = nn(left[...], act[0, m]).astype(out.dtype)


def grad(me, experts, act_all, xt_all, ct_all, dtypes):
    columns, tokens = xt_all.shape
    width = act_all.shape[3]
    part = columns // 3
    left = pl.BlockSpec((part, tokens), lambda i: (i, 0))
    chosen = [
        pl.BlockSpec((1, 3, tokens, width), functools.partial(lambda r, i: (r, 0, 0, 0), r))
        for r in experts
    ]
    return pl.pallas_call(
        functools.partial(grad_kernel, len(experts)),
        grid=(3,),
        out_shape=[jax.ShapeDtypeStruct((3, columns, width), d) for d in dtypes],
        in_specs=[pl.BlockSpec(memory_space=pltpu.SMEM), left, left] + chosen,
        out_specs=[pl.BlockSpec((3, part, width), lambda i: (0, i, 0))] * len(experts),
        compiler_params=pltpu.CompilerParams(vmem_limit_bytes=VMEM_LIMIT),
        cost_estimate=SMALL_COST,
        name="grad",
    )(me, xt_all, ct_all, *[act_all] * len(experts))


def final_kernel(*refs):
    parts, (gate, up, down) = refs[:-3], refs[-3:]
    for m, out in enumerate((gate, up, down)):
        value = parts[0][m].astype(F32)
        for part in parts[1:]:
            value = value + part[m].astype(F32)
        out[0] = value.T if m == 2 else value


def final_sum(parts):
    _, columns, width = parts[0].shape
    part = columns // 3
    tall = jax.ShapeDtypeStruct((1, columns, width), F32)
    return pl.pallas_call(
        final_kernel,
        grid=(3,),
        out_shape=[tall, tall, jax.ShapeDtypeStruct((1, width, columns), F32)],
        in_specs=[pl.BlockSpec((3, part, width), lambda i: (0, i, 0))] * len(parts),
        out_specs=[pl.BlockSpec((1, part, width), lambda i: (0, i, 0))] * 2
        + [pl.BlockSpec((1, width, part), lambda i: (0, 0, i))],
        compiler_params=pltpu.CompilerParams(vmem_limit_bytes=VMEM_LIMIT),
        name="final",
    )(*parts)


def per_device(tokens, gate_probs, expert_ids, cotangent, gate_weight, up_weight, down_weight):
    rows, columns = tokens.shape
    experts = lax.axis_size("expert")
    inner = inner_size(lax.axis_size("fsdp"))
    outer = lax.axis_size("fsdp") // inner
    me = lax.axis_index("expert").astype(jnp.int32).reshape(1)
    place = lax.axis_index("fsdp") // inner

    high = lax.reduce_precision(gate_probs, 8, 7)
    route = jnp.concatenate([high, gate_probs - high, expert_ids.astype(F32)], axis=1).T
    route = jnp.pad(route, ((0, ROUTE_ROWS - route.shape[0]), (0, columns - rows))).astype(BF16)
    own_pay = jnp.concatenate([tokens, cotangent, route], axis=0)

    groups = range(0, outer, 4)
    across = [(g + a, g + b) for g in groups for a, b in ((1, 2), (2, 1))]
    outward = [(g + a, g + b) for g in groups for a, b in ((1, 0), (2, 3))]
    inward = [(b, a) for a, b in outward]
    beside = lambda v: [hop(v, "fsdp", j) for j in range(1, inner)]
    middle = ((place + 1) & 2) != 0

    own_w = jnp.stack([gate_weight[0], up_weight[0], down_weight[0].T])
    near, far = [0, 1], list(range(2, experts))
    size = dict(experts=experts, blocks=4, rows=rows)
    weights = {0: own_w}
    keep, done = {}, {}

    first = hop(own_pay, "fsdp", inner)
    cross1 = line_hop(own_pay, inner, across)
    pays = {0: [own_pay] + beside(own_pay)}
    weights[1] = hop(own_w, "expert", 1)
    for r in far[::2]:
        weights[r] = hop(own_w, "expert", r)
    near_w = [weights[r] for r in near]
    first, cross1, pays[0], near_w = lax.optimization_barrier((first, cross1, pays[0], near_w))

    pays[1] = [first] + beside(first)
    cross2 = line_hop(first, inner, across)
    out2 = line_hop(cross1, inner, outward)
    keep[0], shared = block(me, near, pays[0], near_w, None, None, 0, send_dtype=F32, with_t=True, **size)
    second = jnp.where(middle, cross2, out2)
    second, cross2, cross1, pays[1], shared, tick = lax.optimization_barrier(
        (second, cross2, cross1, pays[1], shared, me)
    )

    pays[2] = [second] + beside(second)
    out3 = line_hop(cross2, inner, outward)
    keep[1], shared = block(tick, near, pays[1], near_w, None, shared, 1, send_dtype=F32, with_t=True, **size)
    third = jnp.where(middle, cross1, out3)
    third, pays[2], shared, tick = lax.optimization_barrier((third, pays[2], shared, me))

    pays[3] = [third] + beside(third)
    keep[2], shared = block(tick, near, pays[2], near_w, None, shared, 2, send_dtype=F32, with_t=True, **size)
    for r in far[::2]:
        weights[r + 1] = hop(after(weights[r], third), "expert", 1)
    far_w = [weights[r] for r in far]
    tick = after(me, shared[0])
    done[0], shared = block(tick, far, pays[0], far_w, keep[0], shared, 0, send_dtype=BF16, with_t=False, **size)
    tick = after(me, shared[0])
    done[3], shared = block(
        tick, near + far, pays[3], near_w + far_w, None, shared, 3, send_dtype=BF16, with_t=True, **size
    )
    tick = after(me, shared[0])
    done[2], shared = block(tick, far, pays[2], far_w, keep[2], shared, 2, send_dtype=BF16, with_t=False, **size)
    tick = after(me, shared[0])
    done[1], shared = block(tick, far, pays[1], far_w, keep[1], shared, 1, send_dtype=BF16, with_t=False, **size)
    act_all, xt_all, ct_all = shared

    small = lambda v: v.astype(BF16)

    def join(k, sends):
        total = done[k][0]
        for got in sends:
            total = total + got.astype(F32)
        return total

    def sends(k, *earlier):
        return [
            hop(after(s, *earlier) if earlier else s, "fsdp", j + 1)
            for j, s in enumerate(done[k][1:])
        ]

    back3, back2 = sends(3), sends(2)
    sum3 = after(join(3, back3), act_all)
    up3 = line_hop(small(sum3), inner, inward)
    back1 = sends(1, sum3)
    order = far[::-1]
    far_grads = grad(after(me, sum3), order, act_all, xt_all, ct_all, [BF16] * len(order))
    far_grads = dict(zip(order, far_grads))
    others = {r: hop(far_grads[r + 1], "expert", 1) for r in far[::2]}
    sum2 = after(join(2, back2) + up3.astype(F32), [far_grads[r] for r in far])
    cross2 = line_hop(small(sum2), inner, across)
    up2 = line_hop(small(sum2), inner, inward)
    back0 = sends(0, sum2)
    arrived = []
    for r in far[::2]:
        chip = small(far_grads[r].astype(F32) + others[r].astype(F32))
        chip = after(chip, sum2)
        arrived.append(hop(chip, "expert", r))
    sum1 = join(1, back1) + cross2.astype(F32)
    sum3 = sum3 + up2.astype(F32)
    sum1, sum3 = lax.optimization_barrier((sum1, sum3, chip))[:2]
    cross3 = line_hop(small(sum3), inner, across)
    last1 = hop(small(sum1), "fsdp", inner)
    near_grads = grad(after(me, sum1, sum3), near[::-1], act_all, xt_all, ct_all, [BF16, F32])
    chip = near_grads[1] + hop(near_grads[0], "expert", 1).astype(F32)
    sum0 = join(0, back0) + cross3.astype(F32) + last1.astype(F32)
    mixed, d_tokens = small(sum0[:rows]), small(sum0[rows : 2 * rows])
    d_gates = sum0[2 * rows : 2 * rows + 2, :rows].T
    gate, up, down = final_sum([chip] + arrived)
    return mixed, d_tokens, d_gates, gate, up, down


def solution(mesh):
    tok = P(("expert", "fsdp"), None)
    col = P("expert", None, "fsdp")
    row = P("expert", "fsdp", None)
    return jax.shard_map(
        per_device,
        mesh=mesh,
        in_specs=(tok, tok, tok, tok, col, col, row),
        out_specs=(tok, tok, tok, col, col, row),
        check_vma=False,
    )
```

```python
import functools

import jax
import jax.numpy as jnp
from jax import lax
from jax.experimental import pallas as pl
from jax.experimental.pallas import tpu as pltpu
from jax.sharding import PartitionSpec as P

F32, BF16 = jnp.float32, jnp.bfloat16
CONTRACT_COLS = (((1,), (1,)), ((), ()))
ROUTE_ROWS = 8
VMEM_LIMIT = 24 * 1024 * 1024
BLOCK_VMEM = 56 * 1024 * 1024
SMALL_COST = pl.CostEstimate(flops=1000, bytes_accessed=1000, transcendentals=0)
ANY = pl.BlockSpec(memory_space=pl.ANY)
VMEM = pl.BlockSpec(memory_space=pltpu.VMEM)


def hop(value, axis, step):
    return lax.ppermute(value, axis, [(i, i ^ step) for i in range(lax.axis_size(axis))])


def inner_size(size):
    inner = 1
    while inner * inner * 4 <= size:
        inner *= 2
    return inner


def after(value, *earlier):
    return lax.optimization_barrier((value,) + earlier)[0]


def nt(a, b):
    return lax.dot_general(a, b, CONTRACT_COLS, preferred_element_type=F32)


def nn(a, b):
    return jnp.dot(a, b, preferred_element_type=F32)


def block_kernel(steps, shards, rows, at, has_acc, with_t, aliased, me_ref, *refs):
    refs = list(refs)
    take = lambda n: [refs.pop(0) for _ in range(n)]
    pays, weights = take(shards), [take(3) for _ in steps]
    accs = take(shards) if has_acc else []
    take(aliased)
    outs = take(shards)
    (act_all,) = take(1)
    t_all = take(2) if with_t else []
    x_ref, c_ref, mixed_ref, back_ref, w_ref, act_ref = take(6)
    t_refs = take(2) if with_t else []
    acc_refs = take(shards) if has_acc else []
    w_sem, act_sem, t_sem, acc_sem = take(4)
    total = shards * rows
    columns = x_ref.shape[1]
    w_copies = [
        [pltpu.make_async_copy(w[m], w_ref.at[i, m], w_sem.at[i, m]) for m in range(3)]
        for i, w in enumerate(weights)
    ]
    for group in w_copies:
        for m in (0, 1, 2):
            group[m].start()
    acc_copies = [
        pltpu.make_async_copy(a, r, acc_sem.at[j]) for j, (a, r) in enumerate(zip(accs, acc_refs))
    ]
    for copy in acc_copies:
        copy.start()
    for j, pay in enumerate(pays):
        x_ref[j * rows : (j + 1) * rows, :] = pay[0:rows, :]
        c_ref[j * rows : (j + 1) * rows, :] = pay[rows : 2 * rows, :]
    t_copies = []
    if with_t:
        for n, source in enumerate((x_ref, c_ref)):
            t_refs[n][...] = source[...].T
            t_copies.append(
                pltpu.make_async_copy(
                    t_refs[n], t_all[n].at[:, at : at + total], t_sem.at[n]
                )
            )
            t_copies[n].start()
    eye = (
        lax.broadcasted_iota(jnp.int32, (rows, rows), 0)
        == lax.broadcasted_iota(jnp.int32, (rows, rows), 1)
    ).astype(BF16)
    routes = [pay[2 * rows : 2 * rows + ROUTE_ROWS, 0:rows] for pay in pays]
    stand = jnp.concatenate([nt(eye, route) for route in routes], axis=0)
    lying = jnp.concatenate([route.astype(F32) for route in routes], axis=1)
    gates = [jnp.zeros((1, total), F32), jnp.zeros((1, total), F32)]
    act_copies = []
    for i, step in enumerate(steps):
        e = (me_ref[0] ^ step).astype(F32)
        prob = jnp.where(stand[:, 4:5] == e, stand[:, 0:1] + stand[:, 2:3], 0.0)
        prob = prob + jnp.where(stand[:, 5:6] == e, stand[:, 1:2] + stand[:, 3:4], 0.0)
        w_copies[i][0].wait()
        pre_gate = nn(x_ref[...], w_ref[i, 0])
        w_copies[i][1].wait()
        pre_up = nn(x_ref[...], w_ref[i, 1])
        w_copies[i][2].wait()
        d_raw = nn(c_ref[...], w_ref[i, 2])
        sig = jax.nn.sigmoid(pre_gate)
        silu = pre_gate * sig
        hidden = silu * pre_up
        hidden_p = (prob * hidden).astype(BF16)
        product = (hidden * d_raw).astype(BF16)
        sums = nt(jnp.ones((8, product.shape[1]), BF16), product)[0:1]
        for k in range(2):
            gates[k] = gates[k] + jnp.where(lying[4 + k : 5 + k] == e, sums, 0.0)
        d_hidden = prob * d_raw
        d_gate = (d_hidden * pre_up * sig * (1.0 + pre_gate * (1.0 - sig))).astype(BF16)
        d_up = (d_hidden * silu).astype(BF16)
        for m, value in enumerate((d_gate, d_up, hidden_p)):
            act_ref[i, m] = value
            copy = pltpu.make_async_copy(
                act_ref.at[i, m],
                act_all.at[step, m, at : at + total, :],
                act_sem.at[i, m],
            )
            copy.start()
            act_copies.append(copy)
        mixed = nt(hidden_p, w_ref[i, 2])
        back = nt(d_gate, w_ref[i, 0]) + nt(d_up, w_ref[i, 1])
        if i == 0:
            mixed_ref[...] = mixed
            back_ref[...] = back
        else:
            mixed_ref[...] += mixed
            back_ref[...] += back
    for copy in acc_copies:
        copy.wait()
    for j, out in enumerate(outs):
        part = slice(j * rows, (j + 1) * rows)
        mixed, back = mixed_ref[part, :], back_ref[part, :]
        pair = jnp.concatenate(
            [g[:, part] for g in gates] + [jnp.zeros((ROUTE_ROWS - 2, rows), F32)], axis=0
        )
        pair = jnp.concatenate([pair, jnp.zeros((ROUTE_ROWS, columns - rows), F32)], axis=1)
        if has_acc:
            mixed = mixed + acc_refs[j][0:rows, :].astype(F32)
            back = back + acc_refs[j][rows : 2 * rows, :].astype(F32)
            pair = pair + acc_refs[j][2 * rows :, :].astype(F32)
        out[0:rows, :] = mixed.astype(out.dtype)
        out[rows : 2 * rows, :] = back.astype(out.dtype)
        out[2 * rows :, :] = pair.astype(out.dtype)
    for copy in t_copies + act_copies:
        copy.wait()


def block(me, steps, pays, weights, accs, shared, at, *, rows, with_t, experts, tokens):
    shards, count = len(pays), len(steps)
    columns = pays[0].shape[1]
    width = weights[0][0].shape[1]
    total = shards * rows
    outs = [jax.ShapeDtypeStruct(pays[0].shape, BF16)] * shards
    filled = [jax.ShapeDtypeStruct((experts, 3, tokens, width), BF16)]
    if with_t:
        filled += [jax.ShapeDtypeStruct((columns, tokens), BF16)] * 2
    old = list(shared[: len(filled)]) if shared else []
    args = list(pays) + [w for three in weights for w in three] + list(accs or []) + old
    first = 1 + len(args) - len(old)
    scratch = [pltpu.VMEM((total, columns), BF16)] * 2 + [pltpu.VMEM((total, columns), F32)] * 2
    scratch += [pltpu.VMEM((count, 3, columns, width), BF16), pltpu.VMEM((count, 3, total, width), BF16)]
    if with_t:
        scratch += [pltpu.VMEM((columns, total), BF16)] * 2
    if accs:
        scratch += [pltpu.VMEM(a.shape, BF16) for a in accs]
    dma = pltpu.SemaphoreType.DMA
    scratch += [dma((count, 3)), dma((count, 3)), dma((2,)), dma((shards,))]
    res = pl.pallas_call(
        functools.partial(
            block_kernel, tuple(steps), shards, rows, at, bool(accs), with_t, len(old)
        ),
        out_shape=outs + filled,
        in_specs=[pl.BlockSpec(memory_space=pltpu.SMEM)]
        + [VMEM] * shards
        + [ANY] * (len(args) - shards),
        out_specs=[VMEM] * shards + [ANY] * len(filled),
        scratch_shapes=scratch,
        input_output_aliases={first + n: shards + n for n in range(len(old))},
        compiler_params=pltpu.CompilerParams(vmem_limit_bytes=BLOCK_VMEM),
        cost_estimate=SMALL_COST,
        name="block",
    )(me, *args)
    new = list(res[shards:])
    return res[:shards], new + list(shared[len(new) :] if shared else [])


def grad_kernel(parts, count, me_ref, *refs):
    lefts = {}
    refs = list(refs)
    if parts != (2,):
        lefts[0] = lefts[1] = refs.pop(0)
    if 2 in parts:
        lefts[2] = refs.pop(0)
    for act, out in zip(refs[:count], refs[count:]):
        for n, m in enumerate(parts):
            at = m if act.shape[1] == 3 else n
            out[n] = nn(lefts[m][...], act[0, at]).astype(out.dtype)


def grad(me, experts, act_all, xt_all, ct_all, parts):
    columns, tokens = xt_all.shape
    width = act_all.shape[3]
    part = columns // 3
    lefts = ([xt_all] if parts != (2,) else []) + ([ct_all] if 2 in parts else [])
    place = parts[0] // len(parts)
    chosen = [
        pl.BlockSpec((1, len(parts), tokens, width), functools.partial(lambda r, i: (r, place, 0, 0), r))
        for r in experts
    ]
    return pl.pallas_call(
        functools.partial(grad_kernel, parts, len(experts)),
        grid=(3,),
        out_shape=[jax.ShapeDtypeStruct((len(parts), columns, width), BF16)] * len(experts),
        in_specs=[pl.BlockSpec(memory_space=pltpu.SMEM)]
        + [pl.BlockSpec((part, tokens), lambda i: (i, 0))] * len(lefts)
        + chosen,
        out_specs=[pl.BlockSpec((len(parts), part, width), lambda i: (0, i, 0))] * len(experts),
        compiler_params=pltpu.CompilerParams(vmem_limit_bytes=VMEM_LIMIT),
        cost_estimate=SMALL_COST,
        name="grad",
    )(me, *lefts, *[act_all] * len(experts))


def final_kernel(places, turned, count, *refs):
    parts, outs = refs[:count], refs[count:]
    for n, out in enumerate(outs):
        value = parts[0][places[0][n]].astype(F32)
        for part, at in zip(parts[1:], places[1:]):
            value = value + part[at[n]].astype(F32)
        out[0] = value.T if turned else value


def final_sum(parts, places, turned):
    _, columns, width = parts[0].shape
    part = columns // 3
    if turned:
        shape, spec = (1, width, columns), pl.BlockSpec((1, width, part), lambda i: (0, 0, i))
    else:
        shape, spec = (1, columns, width), pl.BlockSpec((1, part, width), lambda i: (0, i, 0))
    return pl.pallas_call(
        functools.partial(final_kernel, places, turned, len(parts)),
        grid=(3,),
        out_shape=[jax.ShapeDtypeStruct(shape, F32)] * len(places[0]),
        in_specs=[pl.BlockSpec((p.shape[0], part, width), lambda i: (0, i, 0)) for p in parts],
        out_specs=[spec] * len(places[0]),
        compiler_params=pltpu.CompilerParams(vmem_limit_bytes=VMEM_LIMIT),
        cost_estimate=SMALL_COST,
        name="final",
    )(*parts)


def per_device(tokens, gate_probs, expert_ids, cotangent, gate_weight, up_weight, down_weight):
    rows, columns = tokens.shape
    experts = lax.axis_size("expert")
    inner = inner_size(lax.axis_size("fsdp"))
    outer = lax.axis_size("fsdp") // inner
    me = lax.axis_index("expert").astype(jnp.int32).reshape(1)

    high = lax.reduce_precision(gate_probs, 8, 7)
    route = jnp.concatenate([high, gate_probs - high, expert_ids.astype(F32)], axis=1).T
    route = jnp.pad(route, ((0, ROUTE_ROWS - route.shape[0]), (0, columns - rows))).astype(BF16)
    own_pay = jnp.concatenate([tokens, cotangent, route], axis=0)

    beside = lambda v: [hop(v, "fsdp", j) for j in range(1, inner)]
    block_rows = inner * rows
    near, far = [0, 1], list(range(2, experts))
    size = dict(experts=experts, tokens=outer * block_rows, rows=rows)
    near_size, far_size = dict(with_t=True, **size), dict(with_t=False, **size)
    own_w = [gate_weight[0], up_weight[0], down_weight[0].T]
    weights = {r: [None] * 3 for r in range(experts)}
    weights[0] = own_w
    keep, done = {}, {}

    first = hop(own_pay, "fsdp", inner)
    second = hop(own_pay, "fsdp", 2 * inner)
    pays = {0: [own_pay] + beside(own_pay)}
    for r in far[::2]:
        weights[r][0] = hop(own_w[0], "expert", r)
    weights[1] = [hop(w, "expert", 1) for w in own_w]
    near_w = [weights[r] for r in near]
    keep[0], shared = block(me, near, pays[0], near_w, None, None, 0, **near_size)
    far_gate = [weights[r][0] for r in far[::2]]
    first, second, far_gate, shared = lax.optimization_barrier((first, second, far_gate, shared))

    pays[1] = [first] + beside(first)
    pays[2] = [second] + beside(second)
    third = hop(second, "fsdp", inner)
    for r, gate in zip(far[::2], far_gate):
        weights[r][0] = gate
        weights[r + 1][0] = hop(gate, "expert", 1)
        weights[r][1] = hop(after(own_w[1], gate), "expert", r)
    far_up = [weights[r][1] for r in far[::2]]
    third, far_up, pays[1], tick = lax.optimization_barrier((third, far_up, pays[1], me))

    pays[3] = [third] + beside(third)
    for r, up in zip(far[::2], far_up):
        weights[r][1] = up
        weights[r + 1][1] = hop(up, "expert", 1)
        weights[r][2] = hop(after(own_w[2], up), "expert", r)
        weights[r + 1][2] = hop(weights[r][2], "expert", 1)
    keep[1], shared = block(tick, near, pays[1], near_w, None, shared, block_rows, **near_size)
    keep[2], shared = block(
        after(me, shared[0]), near, pays[2], near_w, None, shared, 2 * block_rows, **near_size
    )
    far_w = [weights[r] for r in far]
    done[2], shared = block(
        after(me, shared[0]), far, pays[2], far_w, keep[2], shared, 2 * block_rows, **far_size
    )
    done[3], shared = block(
        after(me, shared[0]), near + far, pays[3], near_w + far_w, None, shared, 3 * block_rows,
        **near_size,
    )
    tick = after(me, shared[0])
    if 2 * block_rows <= 512:
        both, shared = block(
            tick, far, pays[0] + pays[1], far_w, list(keep[0]) + list(keep[1]), shared, 0, **far_size
        )
        done[0], done[1] = both[:inner], both[inner:]
    else:
        done[0], shared = block(tick, far, pays[0], far_w, keep[0], shared, 0, **far_size)
        done[1], shared = block(tick, far, pays[1], far_w, keep[1], shared, block_rows, **far_size)
    act_all, xt_all, ct_all = shared

    small = lambda v: v.astype(BF16)

    def join(k, got):
        total = done[k][0].astype(F32)
        for g in got:
            total = total + g.astype(F32)
        return total

    def sends(k, *earlier):
        return [
            hop(after(s, *earlier) if earlier else s, "fsdp", j + 1)
            for j, s in enumerate(done[k][1:])
        ]

    back2, back3 = sends(2), sends(3)
    back2 = after(back2, act_all)
    sum2 = small(join(2, back2))
    home2 = hop(sum2, "fsdp", 2 * inner)
    back1 = sends(1, sum2)
    order = far[::-1]
    far_down = dict(zip(order, grad(after(me, sum2), order, act_all, xt_all, ct_all, (2,))))
    other_down = [hop(far_down[r + 1], "expert", 1) for r in far[::2]]
    tick = after(me, [far_down[r] for r in far])
    far_gu = dict(zip(order, grad(tick, order, act_all, xt_all, ct_all, (0, 1))))
    other_gu = [hop(far_gu[r + 1], "expert", 1) for r in far[::2]]
    gu_list = [far_gu[r] for r in far]
    other_down, back3 = lax.optimization_barrier((other_down, back3, gu_list))[:2]
    arrived_down, arrived_gu = [], []
    for r, other in zip(far[::2], other_down):
        chip = small(far_down[r].astype(F32) + other.astype(F32))
        arrived_down.append(hop(chip, "expert", r))
    sum3 = small(join(3, back3))
    home3 = hop(sum3, "fsdp", 3 * inner)
    other_gu = after(other_gu, sum3, chip)
    for r, other in zip(far[::2], other_gu):
        chip = small(far_gu[r].astype(F32) + other.astype(F32))
        arrived_gu.append(hop(chip, "expert", r))
    back1 = after(back1, chip)
    sum1 = small(join(1, back1))
    home1 = hop(after(sum1, home2), "fsdp", inner)
    back0 = sends(0, sum1)
    near_grads = grad(after(me, sum1, arrived_down), near[::-1], act_all, xt_all, ct_all, (0, 1, 2))
    chip = near_grads[1].astype(F32) + hop(near_grads[0], "expert", 1).astype(F32)
    chip = small(chip)
    (down,) = final_sum([chip] + arrived_down, [(2,)] + [(0,)] * len(arrived_down), True)
    sum0 = join(0, back0)
    for got in (home1, home2, home3):
        sum0 = sum0 + got.astype(F32)
    mixed, d_tokens = small(sum0[:rows]), small(sum0[rows : 2 * rows])
    d_gates = sum0[2 * rows : 2 * rows + 2, :rows].T
    gate, up = final_sum([chip] + arrived_gu, [(0, 1)] * (1 + len(arrived_gu)), False)
    return mixed, d_tokens, d_gates, gate, up, down


def solution(mesh):
    tok = P(("expert", "fsdp"), None)
    col = P("expert", None, "fsdp")
    row = P("expert", "fsdp", None)
    return jax.shard_map(
        per_device,
        mesh=mesh,
        in_specs=(tok, tok, tok, tok, col, col, row),
        out_specs=(tok, tok, tok, col, col, row),
        check_vma=False,
    )
```

```python
import functools

import jax
import jax.numpy as jnp
from jax import lax
from jax.experimental import pallas as pl
from jax.experimental.pallas import tpu as pltpu
from jax.sharding import PartitionSpec as P

F32, BF16 = jnp.float32, jnp.bfloat16
CONTRACT_COLS = (((1,), (1,)), ((), ()))
ROUTE_ROWS = 8
VMEM_LIMIT = 24 * 1024 * 1024
BLOCK_VMEM = 56 * 1024 * 1024
SMALL_COST = pl.CostEstimate(flops=1000, bytes_accessed=1000, transcendentals=0)
ANY = pl.BlockSpec(memory_space=pl.ANY)
VMEM = pl.BlockSpec(memory_space=pltpu.VMEM)


def hop(value, axis, step):
    return lax.ppermute(value, axis, [(i, i ^ step) for i in range(lax.axis_size(axis))])


def inner_size(size):
    inner = 1
    while inner * inner * 4 <= size:
        inner *= 2
    return inner


def after(value, *earlier):
    return lax.optimization_barrier((value,) + earlier)[0]


def nt(a, b):
    return lax.dot_general(a, b, CONTRACT_COLS, preferred_element_type=F32)


def nn(a, b):
    return jnp.dot(a, b, preferred_element_type=F32)


def block_kernel(steps, packs, rows, places, has_acc, with_t, aliased, me_ref, *refs):
    refs = list(refs)
    take = lambda n: [refs.pop(0) for _ in range(n)]
    shards = len(places)
    pays = []
    for pack, ref in zip(packs, take(len(packs))):
        pays += [ref] if pack is None else [ref.at[i] for i in pack]
    weights = [take(2) for _ in steps]
    accs = take(shards) if has_acc else []
    take(aliased)
    outs = take(shards)
    (act_all,) = take(1)
    t_all = take(2) if with_t else []
    x_ref, c_ref, gu_ref, down_ref, dgu_ref, hp_ref = take(6)
    t_refs = take(2) if with_t else []
    acc_refs = take(shards) if has_acc else []
    w_sem, act_sem, t_sem, acc_sem = take(4)
    columns = x_ref.shape[1]
    width = hp_ref.shape[1] // len(steps)
    at = lambda n: slice(n * width, (n + 1) * width)
    w_copies = []
    for i, (gu, down) in enumerate(weights):
        targets = (gu_ref.at[:, at(2 * i)], gu_ref.at[:, at(2 * i + 1)], down_ref.at[:, at(i)])
        w_copies.append(
            [
                pltpu.make_async_copy(w, target, w_sem.at[i, m])
                for m, (w, target) in enumerate(zip((gu.at[0], gu.at[1], down), targets))
            ]
        )
    acc_copies = [
        pltpu.make_async_copy(a, r, acc_sem.at[j]) for j, (a, r) in enumerate(zip(accs, acc_refs))
    ]
    for copy in [c for group in w_copies for c in group] + acc_copies:
        copy.start()
    for j, pay in enumerate(pays):
        x_ref[j * rows : (j + 1) * rows, :] = pay[0:rows, :]
        c_ref[j * rows : (j + 1) * rows, :] = pay[rows : 2 * rows, :]
    t_copies = []
    if with_t:
        for n, source in enumerate((x_ref, c_ref)):
            t_refs[n][...] = source[...].T
            for j, place in enumerate(places):
                t_copies.append(
                    pltpu.make_async_copy(
                        t_refs[n].at[:, j * rows : (j + 1) * rows],
                        t_all[n].at[:, place : place + rows],
                        t_sem.at[n, j],
                    )
                )
        for copy in t_copies:
            copy.start()
    eye = (
        lax.broadcasted_iota(jnp.int32, (rows, rows), 0)
        == lax.broadcasted_iota(jnp.int32, (rows, rows), 1)
    ).astype(BF16)
    routes = [pay[2 * rows : 2 * rows + ROUTE_ROWS, 0:rows] for pay in pays]
    stand = jnp.concatenate([nt(eye, route) for route in routes], axis=0)
    lying = jnp.concatenate([route.astype(F32) for route in routes], axis=1)
    gates = [jnp.zeros((1, shards * rows), F32), jnp.zeros((1, shards * rows), F32)]
    act_copies = []
    for i, step in enumerate(steps):
        e = (me_ref[0] ^ step).astype(F32)
        prob = jnp.where(stand[:, 4:5] == e, stand[:, 0:1] + stand[:, 2:3], 0.0)
        prob = prob + jnp.where(stand[:, 5:6] == e, stand[:, 1:2] + stand[:, 3:4], 0.0)
        w_copies[i][0].wait()
        pre_gate = nn(x_ref[...], gu_ref[:, at(2 * i)])
        w_copies[i][1].wait()
        pre_up = nn(x_ref[...], gu_ref[:, at(2 * i + 1)])
        w_copies[i][2].wait()
        d_raw = nn(c_ref[...], down_ref[:, at(i)])
        sig = jax.nn.sigmoid(pre_gate)
        silu = pre_gate * sig
        hidden = silu * pre_up
        product = (hidden * d_raw).astype(BF16)
        sums = nt(jnp.ones((8, width), BF16), product)[0:1]
        for k in range(2):
            gates[k] = gates[k] + jnp.where(lying[4 + k : 5 + k] == e, sums, 0.0)
        d_hidden = prob * d_raw
        slope = pre_up * sig * (1.0 + pre_gate * (1.0 - sig))
        dgu_ref[:, at(2 * i)] = (d_hidden * slope).astype(BF16)
        dgu_ref[:, at(2 * i + 1)] = (d_hidden * silu).astype(BF16)
        hp_ref[:, at(i)] = (prob * hidden).astype(BF16)
        for m, source in enumerate(
            (dgu_ref.at[:, at(2 * i)], dgu_ref.at[:, at(2 * i + 1)], hp_ref.at[:, at(i)])
        ):
            for j, place in enumerate(places):
                copy = pltpu.make_async_copy(
                    source.at[j * rows : (j + 1) * rows, :],
                    act_all.at[step, m, place : place + rows, :],
                    act_sem.at[i, m, j],
                )
                copy.start()
                act_copies.append(copy)
    for copy in acc_copies:
        copy.wait()
    for half, (left, right) in enumerate(((hp_ref, down_ref), (dgu_ref, gu_ref))):
        value = nt(left[...], right[...])
        for j, out in enumerate(outs):
            part = value[j * rows : (j + 1) * rows]
            if has_acc:
                part = part + acc_refs[j][half * rows : (half + 1) * rows, :].astype(F32)
            out[half * rows : (half + 1) * rows, :] = part.astype(out.dtype)
    for j, out in enumerate(outs):
        pair = jnp.concatenate(
            [g[:, j * rows : (j + 1) * rows] for g in gates]
            + [jnp.zeros((ROUTE_ROWS - 2, rows), F32)],
            axis=0,
        )
        pair = jnp.concatenate([pair, jnp.zeros((ROUTE_ROWS, columns - rows), F32)], axis=1)
        if has_acc:
            pair = pair + acc_refs[j][2 * rows :, :].astype(F32)
        out[2 * rows :, :] = pair.astype(out.dtype)
    for copy in t_copies + act_copies:
        copy.wait()


def block(me, steps, pays, weights, accs, shared, places, *, rows, with_t, experts, tokens):
    shards, count = len(places), len(steps)
    packs = tuple(p[1] if isinstance(p, tuple) else None for p in pays)
    pays = [p[0] if isinstance(p, tuple) else p for p in pays]
    height, columns = pays[0].shape[-2:]
    width = weights[0][1].shape[1]
    total = shards * rows
    outs = [jax.ShapeDtypeStruct((height, columns), BF16)] * shards
    filled = [jax.ShapeDtypeStruct((experts, 3, tokens, width), BF16)]
    if with_t:
        filled += [jax.ShapeDtypeStruct((columns, tokens), BF16)] * 2
    old = list(shared[: len(filled)]) if shared else []
    args = list(pays) + [w for two in weights for w in two] + list(accs or []) + old
    first = 1 + len(args) - len(old)
    scratch = [pltpu.VMEM((total, columns), BF16)] * 2
    scratch += [pltpu.VMEM((columns, n * count * width), BF16) for n in (2, 1)]
    scratch += [pltpu.VMEM((total, n * count * width), BF16) for n in (2, 1)]
    if with_t:
        scratch += [pltpu.VMEM((columns, total), BF16)] * 2
    if accs:
        scratch += [pltpu.VMEM(a.shape, BF16) for a in accs]
    dma = pltpu.SemaphoreType.DMA
    scratch += [dma((count, 3)), dma((count, 3, shards)), dma((2, shards)), dma((shards,))]
    res = pl.pallas_call(
        functools.partial(
            block_kernel, tuple(steps), packs, rows, tuple(places), bool(accs), with_t, len(old)
        ),
        out_shape=outs + filled,
        in_specs=[pl.BlockSpec(memory_space=pltpu.SMEM)]
        + [VMEM] * len(pays)
        + [ANY] * (len(args) - len(pays)),
        out_specs=[VMEM] * shards + [ANY] * len(filled),
        scratch_shapes=scratch,
        input_output_aliases={first + n: shards + n for n in range(len(old))},
        compiler_params=pltpu.CompilerParams(vmem_limit_bytes=BLOCK_VMEM),
        cost_estimate=SMALL_COST,
        name="block",
    )(me, *args)
    new = list(res[shards:])
    return res[:shards], new + list(shared[len(new) :] if shared else [])


def grad_kernel(parts, count, me_ref, *refs):
    lefts = {}
    refs = list(refs)
    if parts != (2,):
        lefts[0] = lefts[1] = refs.pop(0)
    if 2 in parts:
        lefts[2] = refs.pop(0)
    for act, out in zip(refs[:count], refs[count:]):
        for n, m in enumerate(parts):
            at = m if act.shape[1] == 3 else n
            out[n] = nn(lefts[m][...], act[0, at]).astype(out.dtype)


def grad(me, experts, act_all, xt_all, ct_all, parts):
    columns, tokens = xt_all.shape
    width = act_all.shape[3]
    part = columns // 3
    lefts = ([xt_all] if parts != (2,) else []) + ([ct_all] if 2 in parts else [])
    place = parts[0] // len(parts)
    chosen = [
        pl.BlockSpec((1, len(parts), tokens, width), functools.partial(lambda r, i: (r, place, 0, 0), r))
        for r in experts
    ]
    return pl.pallas_call(
        functools.partial(grad_kernel, parts, len(experts)),
        grid=(3,),
        out_shape=[jax.ShapeDtypeStruct((len(parts), columns, width), BF16)] * len(experts),
        in_specs=[pl.BlockSpec(memory_space=pltpu.SMEM)]
        + [pl.BlockSpec((part, tokens), lambda i: (i, 0))] * len(lefts)
        + chosen,
        out_specs=[pl.BlockSpec((len(parts), part, width), lambda i: (0, i, 0))] * len(experts),
        compiler_params=pltpu.CompilerParams(vmem_limit_bytes=VMEM_LIMIT),
        cost_estimate=SMALL_COST,
        name="grad",
    )(me, *lefts, *[act_all] * len(experts))


def final_kernel(places, turned, count, *refs):
    parts, outs = refs[:count], refs[count:]
    for n, out in enumerate(outs):
        value = parts[0][places[0][n]].astype(F32)
        for part, at in zip(parts[1:], places[1:]):
            value = value + part[at[n]].astype(F32)
        out[0] = value.T if turned else value


def final_sum(parts, places, turned):
    _, columns, width = parts[0].shape
    part = columns // 3
    if turned:
        shape, spec = (1, width, columns), pl.BlockSpec((1, width, part), lambda i: (0, 0, i))
    else:
        shape, spec = (1, columns, width), pl.BlockSpec((1, part, width), lambda i: (0, i, 0))
    return pl.pallas_call(
        functools.partial(final_kernel, places, turned, len(parts)),
        grid=(3,),
        out_shape=[jax.ShapeDtypeStruct(shape, F32)] * len(places[0]),
        in_specs=[pl.BlockSpec((p.shape[0], part, width), lambda i: (0, i, 0)) for p in parts],
        out_specs=[spec] * len(places[0]),
        compiler_params=pltpu.CompilerParams(vmem_limit_bytes=VMEM_LIMIT),
        cost_estimate=SMALL_COST,
        name="final",
    )(*parts)


def per_device(tokens, gate_probs, expert_ids, cotangent, gate_weight, up_weight, down_weight):
    rows, columns = tokens.shape
    experts = lax.axis_size("expert")
    inner = inner_size(lax.axis_size("fsdp"))
    outer = lax.axis_size("fsdp") // inner
    me = lax.axis_index("expert").astype(jnp.int32).reshape(1)

    high = lax.reduce_precision(gate_probs, 8, 7)
    route = jnp.concatenate([high, gate_probs - high, expert_ids.astype(F32)], axis=1).T
    route = jnp.pad(route, ((0, ROUTE_ROWS - route.shape[0]), (0, columns - rows))).astype(BF16)
    own_pay = jnp.concatenate([tokens, cotangent, route], axis=0)

    beside = lambda v: [hop(v, "fsdp", j) for j in range(1, inner)]
    near, far = [0, 1], list(range(2, experts))
    size = dict(experts=experts, tokens=outer * inner * rows, rows=rows)
    own_w = [jnp.stack([gate_weight[0], up_weight[0]]), down_weight[0].T]
    weights = {r: [None] * 2 for r in range(experts)}
    weights[0] = own_w
    pays, keep, done, shared = {}, {}, {}, None
    place = lambda k, j: (k * inner + j) * rows

    def compute(steps, shards, tick, with_t):
        nonlocal shared
        accs = None if with_t else [keep[s] for s in shards]
        packed, seen = [], {}
        for s in shards:
            p = pays[s]
            if isinstance(p, tuple):
                if id(p[0]) in seen:
                    seen[id(p[0])][1].append(p[1])
                    continue
                p = (p[0], [p[1]])
                seen[id(p[0])] = p
            packed.append(p)
        packed = [(p[0], tuple(p[1])) if isinstance(p, tuple) else p for p in packed]
        if shared:
            tick = after(me, tick, shared[0])
        outs, shared = block(
            tick, steps, packed, [weights[r] for r in steps], accs, shared,
            [place(*s) for s in shards], with_t=with_t, **size,
        )
        for s, out in zip(shards, outs):
            (done if steps[-1] == far[-1] else keep)[s] = out

    row_of = lambda k: [(k, j) for j in range(inner)]

    first = hop(own_pay, "fsdp", inner)
    second = hop(own_pay, "fsdp", 2 * inner)
    for j, p in enumerate([own_pay] + beside(own_pay)):
        pays[0, j] = p
    for r in far[::2]:
        weights[r][0] = hop(own_w[0], "expert", r)
    weights[1] = [hop(w, "expert", 1) for w in own_w]
    compute(near, row_of(0), me, True)
    gus = [weights[r][0] for r in far[::2]]
    first, second, gus, shared = lax.optimization_barrier((first, second, gus, shared))

    pays[1, 0], pays[2, 0] = first, second
    pair = beside(jnp.stack([first, second]))
    for j, p in enumerate(pair):
        pays[1, j + 1], pays[2, j + 1] = (p, 0), (p, 1)
    third = hop(second, "fsdp", inner)
    for r, gu in zip(far[::2], gus):
        weights[r][0] = gu
        weights[r + 1][0] = hop(gu, "expert", 1)
        weights[r][1] = hop(after(own_w[1], gu), "expert", r)
    split = inner == 2
    if split:
        compute(near, [(1, 0), (2, 0)], me, True)
    downs = [weights[r][1] for r in far[::2]]
    gus = [weights[r + 1][0] for r in far[::2]]
    third, downs, gus, shared = lax.optimization_barrier((third, downs, gus, shared))

    for j, p in enumerate([third] + beside(third)):
        pays[3, j] = p
    for r, gu, down in zip(far[::2], gus, downs):
        weights[r][1] = down
        weights[r + 1] = [gu, hop(down, "expert", 1)]
    if split:
        compute(far, row_of(0) + [(1, 0), (2, 0)], me, False)
        compute(near, [(1, 1), (2, 1)], me, True)
        compute(far, [(1, 1), (2, 1)], me, False)
    else:
        compute(far, row_of(0), me, False)
        for k in (1, 2):
            compute(near, row_of(k), me, True)
            compute(far, row_of(k), me, False)
    compute(near + far, row_of(3), me, True)

    small = lambda v: v.astype(BF16)

    def join(k, got):
        total = done[k, 0].astype(F32)
        for g in got:
            total = total + g.astype(F32)
        return total

    def sends(k, *earlier):
        return [
            hop(after(done[k, j], *earlier) if earlier else done[k, j], "fsdp", j)
            for j in range(1, inner)
        ]

    act_all, xt_all, ct_all = shared
    back2, back3 = sends(2), sends(3)
    order = far[::-1]
    far_down = dict(zip(order, grad(after(me, act_all), order, act_all, xt_all, ct_all, (2,))))
    other_down = [hop(far_down[r + 1], "expert", 1) for r in far[::2]]
    tick = after(me, [far_down[r] for r in far])
    far_gu = dict(zip(order, grad(tick, order, act_all, xt_all, ct_all, (0, 1))))
    other_gu = [hop(far_gu[r + 1], "expert", 1) for r in far[::2]]
    other_down, back2 = lax.optimization_barrier((other_down, back2, [far_gu[r] for r in far]))[:2]
    arrived_down, arrived_gu = [], []
    for r, other in zip(far[::2], other_down):
        chip = small(far_down[r].astype(F32) + other.astype(F32))
        arrived_down.append(hop(chip, "expert", r))
    back1 = sends(1, back2, chip)
    sum3 = small(join(3, after(back3, chip)))
    up3 = hop(sum3, "fsdp", inner)
    near_grads = grad(after(me, sum3), near[::-1], act_all, xt_all, ct_all, (0, 1, 2))
    up3, back1, arrived_down, other_gu, near_grads = lax.optimization_barrier(
        (up3, back1, arrived_down, other_gu, near_grads)
    )
    sum2 = small(join(2, back2 + [up3]))
    home2 = hop(sum2, "fsdp", 2 * inner)
    sum1 = small(join(1, back1))
    home1 = hop(sum1, "fsdp", inner)
    back0 = sends(0, back1)
    for r, other in zip(far[::2], other_gu):
        chip = small(far_gu[r].astype(F32) + other.astype(F32))
        arrived_gu.append(hop(chip, "expert", r))
    other_near = hop(near_grads[0], "expert", 1)
    sum0 = join(0, back0)
    for got in (home1, home2):
        sum0 = sum0 + got.astype(F32)
    chip = small(near_grads[1].astype(F32) + other_near.astype(F32))
    (down,) = final_sum([chip] + arrived_down, [(2,)] + [(0,)] * len(arrived_down), True)
    mixed, d_tokens = small(sum0[:rows]), small(sum0[rows : 2 * rows])
    d_gates = sum0[2 * rows : 2 * rows + 2, :rows].T
    gate, up = final_sum([chip] + arrived_gu, [(0, 1)] * (1 + len(arrived_gu)), False)
    return mixed, d_tokens, d_gates, gate, up, down


def solution(mesh):
    tok = P(("expert", "fsdp"), None)
    col = P("expert", None, "fsdp")
    row = P("expert", "fsdp", None)
    return jax.shard_map(
        per_device,
        mesh=mesh,
        in_specs=(tok, tok, tok, tok, col, col, row),
        out_specs=(tok, tok, tok, col, col, row),
        check_vma=False,
    )
```

```python
import functools

import jax
import jax.numpy as jnp
from jax import lax
from jax.experimental import pallas as pl
from jax.experimental.pallas import tpu as pltpu
from jax.sharding import PartitionSpec as P

F32, BF16 = jnp.float32, jnp.bfloat16
CONTRACT_COLS = (((1,), (1,)), ((), ()))
ROUTE_ROWS = 8
VMEM_LIMIT = 24 * 1024 * 1024
GRAD_VMEM = 56 * 1024 * 1024
BLOCK_VMEM = 56 * 1024 * 1024
SMALL_COST = pl.CostEstimate(flops=1000, bytes_accessed=1000, transcendentals=0)
ANY = pl.BlockSpec(memory_space=pl.ANY)
VMEM = pl.BlockSpec(memory_space=pltpu.VMEM)


def hop(value, axis, step):
    return lax.ppermute(value, axis, [(i, i ^ step) for i in range(lax.axis_size(axis))])


def inner_size(size):
    inner = 1
    while inner * inner * 4 <= size:
        inner *= 2
    return inner


def after(value, *earlier):
    return lax.optimization_barrier((value,) + earlier)[0]


def nt(a, b):
    return lax.dot_general(a, b, CONTRACT_COLS, preferred_element_type=F32)


def nn(a, b):
    return jnp.dot(a, b, preferred_element_type=F32)


def block_kernel(steps, packs, rows, places, has_acc, with_t, aliased, me_ref, *refs):
    refs = list(refs)
    take = lambda n: [refs.pop(0) for _ in range(n)]
    shards = len(places)
    pays = []
    for pack, ref in zip(packs, take(len(packs))):
        pays += [ref] if pack is None else [ref.at[i] for i in pack]
    weights = [take(2) for _ in steps]
    accs = take(shards) if has_acc else []
    take(aliased)
    outs = take(shards)
    (act_all,) = take(1)
    t_all = take(2) if with_t else []
    x_ref, c_ref, gu_ref, down_ref, dgu_ref, hp_ref = take(6)
    t_refs = take(2) if with_t else []
    acc_refs = take(shards) if has_acc else []
    w_sem, act_sem, t_sem, acc_sem = take(4)
    columns = x_ref.shape[1]
    width = hp_ref.shape[1] // len(steps)
    at = lambda n: slice(n * width, (n + 1) * width)
    w_copies = []
    for i, (gu, down) in enumerate(weights):
        targets = (gu_ref.at[:, at(2 * i)], gu_ref.at[:, at(2 * i + 1)], down_ref.at[:, at(i)])
        w_copies.append(
            [
                pltpu.make_async_copy(w, target, w_sem.at[i, m])
                for m, (w, target) in enumerate(zip((gu.at[0], gu.at[1], down), targets))
            ]
        )
    acc_copies = [
        pltpu.make_async_copy(a, r, acc_sem.at[j]) for j, (a, r) in enumerate(zip(accs, acc_refs))
    ]
    for copy in [c for group in w_copies for c in group] + acc_copies:
        copy.start()
    for j, pay in enumerate(pays):
        x_ref[j * rows : (j + 1) * rows, :] = pay[0:rows, :]
        c_ref[j * rows : (j + 1) * rows, :] = pay[rows : 2 * rows, :]
    t_copies = []
    if with_t:
        for n, source in enumerate((x_ref, c_ref)):
            t_refs[n][...] = source[...].T
            for j, place in enumerate(places):
                t_copies.append(
                    pltpu.make_async_copy(
                        t_refs[n].at[:, j * rows : (j + 1) * rows],
                        t_all[n].at[:, place : place + rows],
                        t_sem.at[n, j],
                    )
                )
        for copy in t_copies:
            copy.start()
    eye = (
        lax.broadcasted_iota(jnp.int32, (rows, rows), 0)
        == lax.broadcasted_iota(jnp.int32, (rows, rows), 1)
    ).astype(BF16)
    routes = [pay[2 * rows : 2 * rows + ROUTE_ROWS, 0:rows] for pay in pays]
    stand = jnp.concatenate([nt(eye, route) for route in routes], axis=0)
    lying = jnp.concatenate([route.astype(F32) for route in routes], axis=1)
    gates = [jnp.zeros((1, shards * rows), F32), jnp.zeros((1, shards * rows), F32)]
    act_copies = []
    for i, step in enumerate(steps):
        e = (me_ref[0] ^ step).astype(F32)
        prob = jnp.where(stand[:, 4:5] == e, stand[:, 0:1] + stand[:, 2:3], 0.0)
        prob = prob + jnp.where(stand[:, 5:6] == e, stand[:, 1:2] + stand[:, 3:4], 0.0)
        w_copies[i][0].wait()
        pre_gate = nn(x_ref[...], gu_ref[:, at(2 * i)])
        w_copies[i][1].wait()
        pre_up = nn(x_ref[...], gu_ref[:, at(2 * i + 1)])
        w_copies[i][2].wait()
        d_raw = nn(c_ref[...], down_ref[:, at(i)])
        sig = jax.nn.sigmoid(pre_gate)
        silu = pre_gate * sig
        hidden = silu * pre_up
        product = (hidden * d_raw).astype(BF16)
        sums = nt(jnp.ones((8, width), BF16), product)[0:1]
        for k in range(2):
            gates[k] = gates[k] + jnp.where(lying[4 + k : 5 + k] == e, sums, 0.0)
        d_hidden = prob * d_raw
        slope = pre_up * sig * (1.0 + pre_gate * (1.0 - sig))
        dgu_ref[:, at(2 * i)] = (d_hidden * slope).astype(BF16)
        dgu_ref[:, at(2 * i + 1)] = (d_hidden * silu).astype(BF16)
        hp_ref[:, at(i)] = (prob * hidden).astype(BF16)
        for m, source in enumerate(
            (dgu_ref.at[:, at(2 * i)], dgu_ref.at[:, at(2 * i + 1)], hp_ref.at[:, at(i)])
        ):
            for j, place in enumerate(places):
                copy = pltpu.make_async_copy(
                    source.at[j * rows : (j + 1) * rows, :],
                    act_all.at[step, m, place : place + rows, :],
                    act_sem.at[i, m, j],
                )
                copy.start()
                act_copies.append(copy)
    for copy in acc_copies:
        copy.wait()
    for half, (left, right) in enumerate(((hp_ref, down_ref), (dgu_ref, gu_ref))):
        value = nt(left[...], right[...])
        for j, out in enumerate(outs):
            part = value[j * rows : (j + 1) * rows]
            if has_acc:
                part = part + acc_refs[j][half * rows : (half + 1) * rows, :].astype(F32)
            out[half * rows : (half + 1) * rows, :] = part.astype(out.dtype)
    for j, out in enumerate(outs):
        pair = jnp.concatenate(
            [g[:, j * rows : (j + 1) * rows] for g in gates]
            + [jnp.zeros((ROUTE_ROWS - 2, rows), F32)],
            axis=0,
        )
        pair = jnp.concatenate([pair, jnp.zeros((ROUTE_ROWS, columns - rows), F32)], axis=1)
        if has_acc:
            pair = pair + acc_refs[j][2 * rows :, :].astype(F32)
        out[2 * rows :, :] = pair.astype(out.dtype)
    for copy in t_copies + act_copies:
        copy.wait()


def block(me, steps, pays, weights, accs, shared, places, *, rows, with_t, experts, tokens):
    shards, count = len(places), len(steps)
    packs = tuple(p[1] if isinstance(p, tuple) else None for p in pays)
    pays = [p[0] if isinstance(p, tuple) else p for p in pays]
    height, columns = pays[0].shape[-2:]
    width = weights[0][1].shape[1]
    total = shards * rows
    outs = [jax.ShapeDtypeStruct((height, columns), BF16)] * shards
    filled = [jax.ShapeDtypeStruct((experts, 3, tokens, width), BF16)]
    if with_t:
        filled += [jax.ShapeDtypeStruct((columns, tokens), BF16)] * 2
    old = list(shared[: len(filled)]) if shared else []
    args = list(pays) + [w for two in weights for w in two] + list(accs or []) + old
    first = 1 + len(args) - len(old)
    scratch = [pltpu.VMEM((total, columns), BF16)] * 2
    scratch += [pltpu.VMEM((columns, n * count * width), BF16) for n in (2, 1)]
    scratch += [pltpu.VMEM((total, n * count * width), BF16) for n in (2, 1)]
    if with_t:
        scratch += [pltpu.VMEM((columns, total), BF16)] * 2
    if accs:
        scratch += [pltpu.VMEM(a.shape, BF16) for a in accs]
    dma = pltpu.SemaphoreType.DMA
    scratch += [dma((count, 3)), dma((count, 3, shards)), dma((2, shards)), dma((shards,))]
    res = pl.pallas_call(
        functools.partial(
            block_kernel, tuple(steps), packs, rows, tuple(places), bool(accs), with_t, len(old)
        ),
        out_shape=outs + filled,
        in_specs=[pl.BlockSpec(memory_space=pltpu.SMEM)]
        + [VMEM] * len(pays)
        + [ANY] * (len(args) - len(pays)),
        out_specs=[VMEM] * shards + [ANY] * len(filled),
        scratch_shapes=scratch,
        input_output_aliases={first + n: shards + n for n in range(len(old))},
        compiler_params=pltpu.CompilerParams(vmem_limit_bytes=BLOCK_VMEM),
        cost_estimate=SMALL_COST,
        name="block",
    )(me, *args)
    new = list(res[shards:])
    return res[:shards], new + list(shared[len(new) :] if shared else [])


def grad_kernel(parts, count, me_ref, *refs):
    lefts = {}
    refs = list(refs)
    if parts != (2,):
        lefts[0] = lefts[1] = refs.pop(0)
    if 2 in parts:
        lefts[2] = refs.pop(0)
    for act, out in zip(refs[:count], refs[count:]):
        for n, m in enumerate(parts):
            at = m if act.shape[1] == 3 else n
            out[n] = nn(lefts[m][...], act[0, at]).astype(out.dtype)


def grad(me, experts, act_all, xt_all, ct_all, parts):
    columns, tokens = xt_all.shape
    width = act_all.shape[3]
    part = columns // 3
    lefts = ([xt_all] if parts != (2,) else []) + ([ct_all] if 2 in parts else [])
    place = parts[0] // len(parts)
    chosen = [
        pl.BlockSpec((1, len(parts), tokens, width), functools.partial(lambda r, i: (r, place, 0, 0), r))
        for r in experts
    ]
    return pl.pallas_call(
        functools.partial(grad_kernel, parts, len(experts)),
        grid=(3,),
        out_shape=[jax.ShapeDtypeStruct((len(parts), columns, width), BF16)] * len(experts),
        in_specs=[pl.BlockSpec(memory_space=pltpu.SMEM)]
        + [pl.BlockSpec((part, tokens), lambda i: (i, 0))] * len(lefts)
        + chosen,
        out_specs=[pl.BlockSpec((len(parts), part, width), lambda i: (0, i, 0))] * len(experts),
        compiler_params=pltpu.CompilerParams(vmem_limit_bytes=GRAD_VMEM),
        cost_estimate=SMALL_COST,
        name="grad",
    )(me, *lefts, *[act_all] * len(experts))


def final_kernel(places, turned, count, *refs):
    parts, outs = refs[:count], refs[count:]
    for n, out in enumerate(outs):
        value = parts[0][places[0][n]].astype(F32)
        for part, at in zip(parts[1:], places[1:]):
            value = value + part[at[n]].astype(F32)
        out[0] = value.T if turned else value


def final_sum(parts, places, turned):
    _, columns, width = parts[0].shape
    part = columns // 3
    if turned:
        shape, spec = (1, width, columns), pl.BlockSpec((1, width, part), lambda i: (0, 0, i))
    else:
        shape, spec = (1, columns, width), pl.BlockSpec((1, part, width), lambda i: (0, i, 0))
    return pl.pallas_call(
        functools.partial(final_kernel, places, turned, len(parts)),
        grid=(3,),
        out_shape=[jax.ShapeDtypeStruct(shape, F32)] * len(places[0]),
        in_specs=[pl.BlockSpec((p.shape[0], part, width), lambda i: (0, i, 0)) for p in parts],
        out_specs=[spec] * len(places[0]),
        compiler_params=pltpu.CompilerParams(vmem_limit_bytes=VMEM_LIMIT),
        cost_estimate=SMALL_COST,
        name="final",
    )(*parts)


def per_device(tokens, gate_probs, expert_ids, cotangent, gate_weight, up_weight, down_weight):
    rows, columns = tokens.shape
    experts = lax.axis_size("expert")
    inner = inner_size(lax.axis_size("fsdp"))
    outer = lax.axis_size("fsdp") // inner
    me = lax.axis_index("expert").astype(jnp.int32).reshape(1)

    high = lax.reduce_precision(gate_probs, 8, 7)
    route = jnp.concatenate([high, gate_probs - high, expert_ids.astype(F32)], axis=1).T
    route = jnp.pad(route, ((0, ROUTE_ROWS - route.shape[0]), (0, columns - rows))).astype(BF16)
    own_pay = jnp.concatenate([tokens, cotangent, route], axis=0)

    beside = lambda v: [hop(v, "fsdp", j) for j in range(1, inner)]
    near, far = [0, 1], list(range(2, experts))
    size = dict(experts=experts, tokens=outer * inner * rows, rows=rows)
    own_w = [jnp.stack([gate_weight[0], up_weight[0]]), down_weight[0].T]
    weights = {r: [None] * 2 for r in range(experts)}
    weights[0] = own_w
    pays, keep, done, shared = {}, {}, {}, None
    place = lambda k, j: (k * inner + j) * rows

    def compute(steps, shards, tick, with_t):
        nonlocal shared
        accs = None if with_t else [keep[s] for s in shards]
        packed, seen = [], {}
        for s in shards:
            p = pays[s]
            if isinstance(p, tuple):
                if id(p[0]) in seen:
                    seen[id(p[0])][1].append(p[1])
                    continue
                p = (p[0], [p[1]])
                seen[id(p[0])] = p
            packed.append(p)
        packed = [(p[0], tuple(p[1])) if isinstance(p, tuple) else p for p in packed]
        if shared:
            tick = after(me, tick, shared[0])
        outs, shared = block(
            tick, steps, packed, [weights[r] for r in steps], accs, shared,
            [place(*s) for s in shards], with_t=with_t, **size,
        )
        for s, out in zip(shards, outs):
            (done if steps[-1] == far[-1] else keep)[s] = out

    row_of = lambda k: [(k, j) for j in range(inner)]

    first = hop(own_pay, "fsdp", inner)
    second = hop(own_pay, "fsdp", 2 * inner)
    for j, p in enumerate([own_pay] + beside(own_pay)):
        pays[0, j] = p
    for r in far[::2]:
        weights[r][0] = hop(own_w[0], "expert", r)
    weights[1] = [hop(w, "expert", 1) for w in own_w]
    compute(near, row_of(0), me, True)
    gus = [weights[r][0] for r in far[::2]]
    first, second, gus, shared = lax.optimization_barrier((first, second, gus, shared))

    pays[1, 0], pays[2, 0] = first, second
    pair = beside(jnp.stack([first, second]))
    for j, p in enumerate(pair):
        pays[1, j + 1], pays[2, j + 1] = (p, 0), (p, 1)
    third = hop(second, "fsdp", inner)
    for r, gu in zip(far[::2], gus):
        weights[r][0] = gu
        weights[r + 1][0] = hop(gu, "expert", 1)
        weights[r][1] = hop(after(own_w[1], gu), "expert", r)
    split = inner == 2
    if split:
        compute(near, [(1, 0), (2, 0)], me, True)
    downs = [weights[r][1] for r in far[::2]]
    gus = [weights[r + 1][0] for r in far[::2]]
    third, downs, gus, shared = lax.optimization_barrier((third, downs, gus, shared))

    for j, p in enumerate([third] + beside(third)):
        pays[3, j] = p
    for r, gu, down in zip(far[::2], gus, downs):
        weights[r][1] = down
        weights[r + 1] = [gu, hop(down, "expert", 1)]
    if split:
        compute(far, row_of(0) + [(1, 0), (2, 0)], me, False)
        compute(near + far, [(1, 1), (2, 1)], me, True)
    else:
        compute(far, row_of(0), me, False)
        for k in (1, 2):
            compute(near + far, row_of(k), me, True)
    compute(near + far, row_of(3), me, True)

    small = lambda v: v.astype(BF16)

    def join(k, got):
        total = done[k, 0].astype(F32)
        for g in got:
            total = total + g.astype(F32)
        return total

    def sends(k, *earlier):
        return [
            hop(after(done[k, j], *earlier) if earlier else done[k, j], "fsdp", j)
            for j in range(1, inner)
        ]

    act_all, xt_all, ct_all = shared
    back2, back3 = sends(2), sends(3)
    order = far[::-1]
    far_down = dict(zip(order, grad(after(me, act_all), order, act_all, xt_all, ct_all, (2,))))
    other_down = [hop(far_down[r + 1], "expert", 1) for r in far[::2]]
    tick = after(me, [far_down[r] for r in far])
    far_gu = dict(zip(order, grad(tick, order, act_all, xt_all, ct_all, (0, 1))))
    other_gu = [hop(far_gu[r + 1], "expert", 1) for r in far[::2]]
    other_down, back2, back3 = lax.optimization_barrier(
        (other_down, back2, back3, [far_gu[r] for r in far])
    )[:3]
    arrived_down, arrived_gu = [], []
    for r, other in zip(far[::2], other_down):
        chip = small(far_down[r].astype(F32) + other.astype(F32))
        arrived_down.append(hop(chip, "expert", r))
    back1 = sends(1, back2, chip)
    sum3 = small(join(3, after(back3, chip)))
    up3 = hop(sum3, "fsdp", inner)
    near_grads = grad(after(me, sum3), near[::-1], act_all, xt_all, ct_all, (0, 1, 2))
    up3, back1, arrived_down, other_gu, near_grads = lax.optimization_barrier(
        (up3, back1, arrived_down, other_gu, near_grads)
    )
    sum2 = small(join(2, back2 + [up3]))
    home2 = hop(sum2, "fsdp", 2 * inner)
    sum1 = small(join(1, back1))
    home1 = hop(sum1, "fsdp", inner)
    back0 = sends(0, back1)
    for r, other in zip(far[::2], other_gu):
        chip = small(far_gu[r].astype(F32) + other.astype(F32))
        arrived_gu.append(hop(chip, "expert", r))
    other_near = hop(near_grads[0], "expert", 1)
    sum0 = join(0, back0)
    for got in (home1, home2):
        sum0 = sum0 + got.astype(F32)
    chip = small(near_grads[1].astype(F32) + other_near.astype(F32))
    (down,) = final_sum([chip] + arrived_down, [(2,)] + [(0,)] * len(arrived_down), True)
    mixed, d_tokens = small(sum0[:rows]), small(sum0[rows : 2 * rows])
    d_gates = sum0[2 * rows : 2 * rows + 2, :rows].T
    gate, up = final_sum([chip] + arrived_gu, [(0, 1)] * (1 + len(arrived_gu)), False)
    return mixed, d_tokens, d_gates, gate, up, down


def solution(mesh):
    tok = P(("expert", "fsdp"), None)
    col = P("expert", None, "fsdp")
    row = P("expert", "fsdp", None)
    return jax.shard_map(
        per_device,
        mesh=mesh,
        in_specs=(tok, tok, tok, tok, col, col, row),
        out_specs=(tok, tok, tok, col, col, row),
        check_vma=False,
    )
```

```python
import functools

import jax
import jax.numpy as jnp
from jax import lax
from jax.experimental import pallas as pl
from jax.experimental.pallas import tpu as pltpu
from jax.sharding import PartitionSpec as P

F32, BF16 = jnp.float32, jnp.bfloat16
CONTRACT_COLS = (((1,), (1,)), ((), ()))
ROUTE_ROWS = 8
VMEM_LIMIT = 24 * 1024 * 1024
GRAD_VMEM = 56 * 1024 * 1024
BLOCK_VMEM = 56 * 1024 * 1024
SMALL_COST = pl.CostEstimate(flops=1000, bytes_accessed=1000, transcendentals=0)
ANY = pl.BlockSpec(memory_space=pl.ANY)
VMEM = pl.BlockSpec(memory_space=pltpu.VMEM)


def hop(value, axis, step):
    return lax.ppermute(value, axis, [(i, i ^ step) for i in range(lax.axis_size(axis))])


def inner_size(size):
    inner = 1
    while inner * inner * 4 <= size:
        inner *= 2
    return inner


def after(value, *earlier):
    return lax.optimization_barrier((value,) + earlier)[0]


def nt(a, b):
    return lax.dot_general(a, b, CONTRACT_COLS, preferred_element_type=F32)


def nn(a, b):
    return jnp.dot(a, b, preferred_element_type=F32)


def block_kernel(steps, packs, rows, places, has_acc, with_t, aliased, me_ref, *refs):
    refs = list(refs)
    take = lambda n: [refs.pop(0) for _ in range(n)]
    shards = len(places)
    pays = []
    for pack, ref in zip(packs, take(len(packs))):
        pays += [ref] if pack is None else [ref.at[i] for i in pack]
    weights = [take(2) for _ in steps]
    accs = take(shards) if has_acc else []
    take(aliased)
    outs = take(shards)
    (act_all,) = take(1)
    t_all = take(2) if with_t else []
    x_ref, c_ref, gu_ref, down_ref, dgu_ref, hp_ref = take(6)
    t_refs = take(2) if with_t else []
    acc_refs = take(shards) if has_acc else []
    w_sem, act_sem, t_sem, acc_sem = take(4)
    columns = x_ref.shape[1]
    width = hp_ref.shape[1] // len(steps)
    at = lambda n: slice(n * width, (n + 1) * width)
    w_copies = []
    half = columns // 2
    for i, (five, one) in enumerate(weights):
        targets = [gu_ref.at[:, at(2 * i)], gu_ref.at[:, at(2 * i + 1)], down_ref.at[:, at(i)]]
        sources = [five.at[n] for n in range(5)] + [one.at[0]]
        w_copies.append(
            [
                [
                    pltpu.make_async_copy(
                        sources[2 * m + n],
                        targets[m].at[n * half : (n + 1) * half, :],
                        w_sem.at[i, 2 * m + n],
                    )
                    for n in range(2)
                ]
                for m in range(3)
            ]
        )
    acc_copies = [
        pltpu.make_async_copy(a, r, acc_sem.at[j]) for j, (a, r) in enumerate(zip(accs, acc_refs))
    ]
    for copy in [c for group in w_copies for two in group for c in two] + acc_copies:
        copy.start()
    for j, pay in enumerate(pays):
        x_ref[j * rows : (j + 1) * rows, :] = pay[0:rows, :]
        c_ref[j * rows : (j + 1) * rows, :] = pay[rows : 2 * rows, :]
    t_copies = []
    if with_t:
        for n, source in enumerate((x_ref, c_ref)):
            t_refs[n][...] = source[...].T
            for j, place in enumerate(places):
                t_copies.append(
                    pltpu.make_async_copy(
                        t_refs[n].at[:, j * rows : (j + 1) * rows],
                        t_all[n].at[:, place : place + rows],
                        t_sem.at[n, j],
                    )
                )
        for copy in t_copies:
            copy.start()
    eye = (
        lax.broadcasted_iota(jnp.int32, (rows, rows), 0)
        == lax.broadcasted_iota(jnp.int32, (rows, rows), 1)
    ).astype(BF16)
    routes = [pay[2 * rows : 2 * rows + ROUTE_ROWS, 0:rows] for pay in pays]
    stand = jnp.concatenate([nt(eye, route) for route in routes], axis=0)
    lying = jnp.concatenate([route.astype(F32) for route in routes], axis=1)
    gates = [jnp.zeros((1, shards * rows), F32), jnp.zeros((1, shards * rows), F32)]
    act_copies = []
    for i, step in enumerate(steps):
        e = (me_ref[0] ^ step).astype(F32)
        prob = jnp.where(stand[:, 4:5] == e, stand[:, 0:1] + stand[:, 2:3], 0.0)
        prob = prob + jnp.where(stand[:, 5:6] == e, stand[:, 1:2] + stand[:, 3:4], 0.0)
        for copy in w_copies[i][0]:
            copy.wait()
        pre_gate = nn(x_ref[...], gu_ref[:, at(2 * i)])
        for copy in w_copies[i][1]:
            copy.wait()
        pre_up = nn(x_ref[...], gu_ref[:, at(2 * i + 1)])
        for copy in w_copies[i][2]:
            copy.wait()
        d_raw = nn(c_ref[...], down_ref[:, at(i)])
        sig = jax.nn.sigmoid(pre_gate)
        silu = pre_gate * sig
        hidden = silu * pre_up
        product = (hidden * d_raw).astype(BF16)
        sums = nt(jnp.ones((8, width), BF16), product)[0:1]
        for k in range(2):
            gates[k] = gates[k] + jnp.where(lying[4 + k : 5 + k] == e, sums, 0.0)
        d_hidden = prob * d_raw
        slope = pre_up * sig * (1.0 + pre_gate * (1.0 - sig))
        dgu_ref[:, at(2 * i)] = (d_hidden * slope).astype(BF16)
        dgu_ref[:, at(2 * i + 1)] = (d_hidden * silu).astype(BF16)
        hp_ref[:, at(i)] = (prob * hidden).astype(BF16)
        for m, source in enumerate(
            (dgu_ref.at[:, at(2 * i)], dgu_ref.at[:, at(2 * i + 1)], hp_ref.at[:, at(i)])
        ):
            for j, place in enumerate(places):
                copy = pltpu.make_async_copy(
                    source.at[j * rows : (j + 1) * rows, :],
                    act_all.at[step, m, place : place + rows, :],
                    act_sem.at[i, m, j],
                )
                copy.start()
                act_copies.append(copy)
    for copy in acc_copies:
        copy.wait()
    for side, (left, right) in enumerate(((hp_ref, down_ref), (dgu_ref, gu_ref))):
        value = nt(left[...], right[...])
        for j, out in enumerate(outs):
            part = value[j * rows : (j + 1) * rows]
            if has_acc:
                part = part + acc_refs[j][side * rows : (side + 1) * rows, :].astype(F32)
            out[side * rows : (side + 1) * rows, :] = part.astype(out.dtype)
    for j, out in enumerate(outs):
        pair = jnp.concatenate(
            [g[:, j * rows : (j + 1) * rows] for g in gates]
            + [jnp.zeros((ROUTE_ROWS - 2, rows), F32)],
            axis=0,
        )
        pair = jnp.concatenate([pair, jnp.zeros((ROUTE_ROWS, columns - rows), F32)], axis=1)
        if has_acc:
            pair = pair + acc_refs[j][2 * rows :, :].astype(F32)
        out[2 * rows :, :] = pair.astype(out.dtype)
    for copy in t_copies + act_copies:
        copy.wait()


def block(me, steps, pays, weights, accs, shared, places, *, rows, with_t, experts, tokens):
    shards, count = len(places), len(steps)
    packs = tuple(p[1] if isinstance(p, tuple) else None for p in pays)
    pays = [p[0] if isinstance(p, tuple) else p for p in pays]
    height, columns = pays[0].shape[-2:]
    width = weights[0][1].shape[2]
    total = shards * rows
    outs = [jax.ShapeDtypeStruct((height, columns), BF16)] * shards
    filled = [jax.ShapeDtypeStruct((experts, 3, tokens, width), BF16)]
    if with_t:
        filled += [jax.ShapeDtypeStruct((columns, tokens), BF16)] * 2
    old = list(shared[: len(filled)]) if shared else []
    args = list(pays) + [w for two in weights for w in two] + list(accs or []) + old
    first = 1 + len(args) - len(old)
    scratch = [pltpu.VMEM((total, columns), BF16)] * 2
    scratch += [pltpu.VMEM((columns, n * count * width), BF16) for n in (2, 1)]
    scratch += [pltpu.VMEM((total, n * count * width), BF16) for n in (2, 1)]
    if with_t:
        scratch += [pltpu.VMEM((columns, total), BF16)] * 2
    if accs:
        scratch += [pltpu.VMEM(a.shape, BF16) for a in accs]
    dma = pltpu.SemaphoreType.DMA
    scratch += [dma((count, 6)), dma((count, 3, shards)), dma((2, shards)), dma((shards,))]
    res = pl.pallas_call(
        functools.partial(
            block_kernel, tuple(steps), packs, rows, tuple(places), bool(accs), with_t, len(old)
        ),
        out_shape=outs + filled,
        in_specs=[pl.BlockSpec(memory_space=pltpu.SMEM)]
        + [VMEM] * len(pays)
        + [ANY] * (len(args) - len(pays)),
        out_specs=[VMEM] * shards + [ANY] * len(filled),
        scratch_shapes=scratch,
        input_output_aliases={first + n: shards + n for n in range(len(old))},
        compiler_params=pltpu.CompilerParams(vmem_limit_bytes=BLOCK_VMEM),
        cost_estimate=SMALL_COST,
        name="block",
    )(me, *args)
    new = list(res[shards:])
    return res[:shards], new + list(shared[len(new) :] if shared else [])


def grad_kernel(parts, count, me_ref, *refs):
    lefts = {}
    refs = list(refs)
    if parts != (2,):
        lefts[0] = lefts[1] = refs.pop(0)
    if 2 in parts:
        lefts[2] = refs.pop(0)
    for act, out in zip(refs[:count], refs[count:]):
        for n, m in enumerate(parts):
            at = m if act.shape[1] == 3 else n
            out[n] = nn(lefts[m][...], act[0, at]).astype(out.dtype)


def grad(me, experts, act_all, xt_all, ct_all, parts):
    columns, tokens = xt_all.shape
    width = act_all.shape[3]
    part = columns // 3
    lefts = ([xt_all] if parts != (2,) else []) + ([ct_all] if 2 in parts else [])
    place = parts[0] // len(parts)
    chosen = [
        pl.BlockSpec((1, len(parts), tokens, width), functools.partial(lambda r, i: (r, place, 0, 0), r))
        for r in experts
    ]
    return pl.pallas_call(
        functools.partial(grad_kernel, parts, len(experts)),
        grid=(3,),
        out_shape=[jax.ShapeDtypeStruct((len(parts), columns, width), BF16)] * len(experts),
        in_specs=[pl.BlockSpec(memory_space=pltpu.SMEM)]
        + [pl.BlockSpec((part, tokens), lambda i: (i, 0))] * len(lefts)
        + chosen,
        out_specs=[pl.BlockSpec((len(parts), part, width), lambda i: (0, i, 0))] * len(experts),
        compiler_params=pltpu.CompilerParams(vmem_limit_bytes=GRAD_VMEM),
        cost_estimate=SMALL_COST,
        name="grad",
    )(me, *lefts, *[act_all] * len(experts))


def final_kernel(places, turned, count, *refs):
    parts, outs = refs[:count], refs[count:]
    for n, out in enumerate(outs):
        value = parts[0][places[0][n]].astype(F32)
        for part, at in zip(parts[1:], places[1:]):
            value = value + part[at[n]].astype(F32)
        out[0] = value.T if turned else value


def final_sum(parts, places, turned):
    _, columns, width = parts[0].shape
    part = columns // 3
    if turned:
        shape, spec = (1, width, columns), pl.BlockSpec((1, width, part), lambda i: (0, 0, i))
    else:
        shape, spec = (1, columns, width), pl.BlockSpec((1, part, width), lambda i: (0, i, 0))
    return pl.pallas_call(
        functools.partial(final_kernel, places, turned, len(parts)),
        grid=(3,),
        out_shape=[jax.ShapeDtypeStruct(shape, F32)] * len(places[0]),
        in_specs=[pl.BlockSpec((p.shape[0], part, width), lambda i: (0, i, 0)) for p in parts],
        out_specs=[spec] * len(places[0]),
        compiler_params=pltpu.CompilerParams(vmem_limit_bytes=VMEM_LIMIT),
        cost_estimate=SMALL_COST,
        name="final",
    )(*parts)


def per_device(tokens, gate_probs, expert_ids, cotangent, gate_weight, up_weight, down_weight):
    rows, columns = tokens.shape
    experts = lax.axis_size("expert")
    inner = inner_size(lax.axis_size("fsdp"))
    outer = lax.axis_size("fsdp") // inner
    me = lax.axis_index("expert").astype(jnp.int32).reshape(1)

    high = lax.reduce_precision(gate_probs, 8, 7)
    route = jnp.concatenate([high, gate_probs - high, expert_ids.astype(F32)], axis=1).T
    route = jnp.pad(route, ((0, ROUTE_ROWS - route.shape[0]), (0, columns - rows))).astype(BF16)
    own_pay = jnp.concatenate([tokens, cotangent, route], axis=0)

    beside = lambda v: [hop(v, "fsdp", j) for j in range(1, inner)]
    near, far = [0, 1], list(range(2, experts))
    size = dict(experts=experts, tokens=outer * inner * rows, rows=rows)
    halves = lambda w: w.reshape(2, columns // 2, -1)
    turned = halves(after(down_weight[0], own_pay).T)
    own_w = [
        jnp.concatenate([halves(gate_weight[0]), halves(up_weight[0]), turned[:1]]),
        turned[1:],
    ]
    weights = {r: [None] * 2 for r in range(experts)}
    weights[0] = own_w
    pays, keep, done, shared = {}, {}, {}, None
    place = lambda k, j: (k * inner + j) * rows

    def compute(steps, shards, tick, with_t):
        nonlocal shared
        accs = None if with_t else [keep[s] for s in shards]
        packed, seen = [], {}
        for s in shards:
            p = pays[s]
            if isinstance(p, tuple):
                if id(p[0]) in seen:
                    seen[id(p[0])][1].append(p[1])
                    continue
                p = (p[0], [p[1]])
                seen[id(p[0])] = p
            packed.append(p)
        packed = [(p[0], tuple(p[1])) if isinstance(p, tuple) else p for p in packed]
        if shared:
            tick = after(me, tick, shared[0])
        outs, shared = block(
            tick, steps, packed, [weights[r] for r in steps], accs, shared,
            [place(*s) for s in shards], with_t=with_t, **size,
        )
        for s, out in zip(shards, outs):
            (done if steps[-1] == far[-1] else keep)[s] = out

    row_of = lambda k: [(k, j) for j in range(inner)]

    first = hop(own_pay, "fsdp", inner)
    second = hop(own_pay, "fsdp", 2 * inner)
    for j, p in enumerate([own_pay] + beside(own_pay)):
        pays[0, j] = p
    for r in far[::2]:
        weights[r][0] = hop(own_w[0], "expert", r)
    weights[1] = [hop(w, "expert", 1) for w in own_w]
    compute(near, row_of(0), me, True)
    gus = [weights[r][0] for r in far[::2]]
    first, second, gus, shared = lax.optimization_barrier((first, second, gus, shared))

    pays[1, 0], pays[2, 0] = first, second
    pair = beside(jnp.stack([first, second]))
    for j, p in enumerate(pair):
        pays[1, j + 1], pays[2, j + 1] = (p, 0), (p, 1)
    third = hop(second, "fsdp", inner)
    for r, gu in zip(far[::2], gus):
        weights[r][0] = gu
        weights[r + 1][0] = hop(gu, "expert", 1)
        weights[r][1] = hop(after(own_w[1], gu), "expert", r)
    split = inner == 2
    if split:
        compute(near, [(1, 0), (2, 0)], me, True)
    downs = [weights[r][1] for r in far[::2]]
    gus = [weights[r + 1][0] for r in far[::2]]
    downs, gus, shared = lax.optimization_barrier((downs, gus, shared))
    for r, gu, down in zip(far[::2], gus, downs):
        weights[r][1] = down
        weights[r + 1] = [gu, hop(down, "expert", 1)]

    if split:
        compute(far, row_of(0) + [(1, 0), (2, 0)], me, False)
    else:
        compute(far, row_of(0), me, False)
    third, shared = lax.optimization_barrier((third, shared))
    for j, p in enumerate([third] + beside(third)):
        pays[3, j] = p
    if split:
        compute(near + far, [(1, 1), (2, 1)], me, True)
    else:
        for k in (1, 2):
            compute(near + far, row_of(k), me, True)
    compute(near + far, row_of(3), me, True)

    small = lambda v: v.astype(BF16)

    def join(k, got):
        total = done[k, 0].astype(F32)
        for g in got:
            total = total + g.astype(F32)
        return total

    def sends(k, *earlier):
        return [
            hop(after(done[k, j], *earlier) if earlier else done[k, j], "fsdp", j)
            for j in range(1, inner)
        ]

    act_all, xt_all, ct_all = shared
    back2, back3 = sends(2), sends(3)
    order = far[::-1]
    far_down = dict(zip(order, grad(after(me, act_all), order, act_all, xt_all, ct_all, (2,))))
    other_down = [hop(far_down[r + 1], "expert", 1) for r in far[::2]]
    tick = after(me, [far_down[r] for r in far])
    far_gu = dict(zip(order, grad(tick, order, act_all, xt_all, ct_all, (0, 1))))
    other_gu = [hop(far_gu[r + 1], "expert", 1) for r in far[::2]]
    other_down, back2, back3 = lax.optimization_barrier(
        (other_down, back2, back3, [far_gu[r] for r in far])
    )[:3]
    arrived_down, arrived_gu = [], []
    for r, other in zip(far[::2], other_down):
        chip = small(far_down[r].astype(F32) + other.astype(F32))
        arrived_down.append(hop(chip, "expert", r))
    back1 = sends(1, back2, chip)
    sum3 = small(join(3, after(back3, chip)))
    up3 = hop(sum3, "fsdp", inner)
    near_grads = grad(after(me, sum3), near[::-1], act_all, xt_all, ct_all, (0, 1, 2))
    other_gu = after(other_gu, near_grads)
    chips = [
        small(far_gu[r].astype(F32) + other.astype(F32)) for r, other in zip(far[::2], other_gu)
    ]
    up3, back1, arrived_down, chips, near_grads = lax.optimization_barrier(
        (up3, back1, arrived_down, chips, near_grads)
    )
    arrived_gu = [hop(chip, "expert", r) for r, chip in zip(far[::2], chips)]
    other_near = hop(near_grads[0], "expert", 1)
    sum2 = small(join(2, back2 + [up3]))
    home2 = hop(sum2, "fsdp", 2 * inner)
    sum1 = small(join(1, after(back1, sum2)))
    home1 = hop(sum1, "fsdp", inner)
    back0 = sends(0, sum1)
    chip = small(near_grads[1].astype(F32) + other_near.astype(F32))
    (down,) = final_sum([chip] + arrived_down, [(2,)] + [(0,)] * len(arrived_down), True)
    sum0 = join(0, after(back0, down))
    for got in (home1, home2):
        sum0 = sum0 + got.astype(F32)
    mixed, d_tokens = small(sum0[:rows]), small(sum0[rows : 2 * rows])
    d_gates = sum0[2 * rows : 2 * rows + 2, :rows].T
    gate, up = final_sum([chip] + arrived_gu, [(0, 1)] * (1 + len(arrived_gu)), False)
    return mixed, d_tokens, d_gates, gate, up, down


def solution(mesh):
    tok = P(("expert", "fsdp"), None)
    col = P("expert", None, "fsdp")
    row = P("expert", "fsdp", None)
    return jax.shard_map(
        per_device,
        mesh=mesh,
        in_specs=(tok, tok, tok, tok, col, col, row),
        out_specs=(tok, tok, tok, col, col, row),
        check_vma=False,
    )
```

```python
import functools

import jax
import jax.numpy as jnp
from jax import lax
from jax.experimental import pallas as pl
from jax.experimental.pallas import tpu as pltpu
from jax.sharding import PartitionSpec as P

F32, BF16 = jnp.float32, jnp.bfloat16
CONTRACT_COLS = (((1,), (1,)), ((), ()))
ROUTE_ROWS = 8
VMEM_LIMIT = 24 * 1024 * 1024
GRAD_VMEM = 56 * 1024 * 1024
BLOCK_VMEM = 56 * 1024 * 1024
SMALL_COST = pl.CostEstimate(flops=1000, bytes_accessed=1000, transcendentals=0)
ANY = pl.BlockSpec(memory_space=pl.ANY)
VMEM = pl.BlockSpec(memory_space=pltpu.VMEM)


def hop(value, axis, step):
    return lax.ppermute(value, axis, [(i, i ^ step) for i in range(lax.axis_size(axis))])


def inner_size(size):
    inner = 1
    while inner * inner * 4 <= size:
        inner *= 2
    return inner


def after(value, *earlier):
    return lax.optimization_barrier((value,) + earlier)[0]


def nt(a, b):
    return lax.dot_general(a, b, CONTRACT_COLS, preferred_element_type=F32)


def nn(a, b):
    return jnp.dot(a, b, preferred_element_type=F32)


def block_kernel(steps, packs, rows, places, has_acc, with_t, aliased, me_ref, *refs):
    refs = list(refs)
    take = lambda n: [refs.pop(0) for _ in range(n)]
    shards = len(places)
    pays = []
    for pack, ref in zip(packs, take(len(packs))):
        pays += [ref] if pack is None else [ref.at[i] for i in pack]
    weights = [take(2) for _ in steps]
    accs = take(shards) if has_acc else []
    take(aliased)
    outs = take(shards)
    (act_all,) = take(1)
    t_all = take(2) if with_t else []
    x_ref, c_ref, gu_ref, down_ref, dgu_ref, hp_ref = take(6)
    t_refs = take(2) if with_t else []
    acc_refs = take(shards) if has_acc else []
    w_sem, act_sem, t_sem, acc_sem = take(4)
    columns = x_ref.shape[1]
    width = hp_ref.shape[1] // len(steps)
    at = lambda n: slice(n * width, (n + 1) * width)
    w_copies = []
    half = columns // 2
    for i, (five, one) in enumerate(weights):
        targets = [gu_ref.at[:, at(2 * i)], gu_ref.at[:, at(2 * i + 1)], down_ref.at[:, at(i)]]
        sources = [five.at[n] for n in range(5)] + [one.at[0]]
        w_copies.append(
            [
                [
                    pltpu.make_async_copy(
                        sources[2 * m + n],
                        targets[m].at[n * half : (n + 1) * half, :],
                        w_sem.at[i, 2 * m + n],
                    )
                    for n in range(2)
                ]
                for m in range(3)
            ]
        )
    acc_copies = [
        pltpu.make_async_copy(a, r, acc_sem.at[j]) for j, (a, r) in enumerate(zip(accs, acc_refs))
    ]
    for copy in [c for group in w_copies for two in group for c in two] + acc_copies:
        copy.start()
    for j, pay in enumerate(pays):
        x_ref[j * rows : (j + 1) * rows, :] = pay[0:rows, :]
        c_ref[j * rows : (j + 1) * rows, :] = pay[rows : 2 * rows, :]
    t_copies = []
    if with_t:
        for n, source in enumerate((x_ref, c_ref)):
            t_refs[n][...] = source[...].T
            for j, place in enumerate(places):
                t_copies.append(
                    pltpu.make_async_copy(
                        t_refs[n].at[:, j * rows : (j + 1) * rows],
                        t_all[n].at[:, place : place + rows],
                        t_sem.at[n, j],
                    )
                )
        for copy in t_copies:
            copy.start()
    eye = (
        lax.broadcasted_iota(jnp.int32, (rows, rows), 0)
        == lax.broadcasted_iota(jnp.int32, (rows, rows), 1)
    ).astype(BF16)
    routes = [pay[2 * rows : 2 * rows + ROUTE_ROWS, 0:rows] for pay in pays]
    stand = jnp.concatenate([nt(eye, route) for route in routes], axis=0)
    lying = jnp.concatenate([route.astype(F32) for route in routes], axis=1)
    gates = [jnp.zeros((1, shards * rows), F32), jnp.zeros((1, shards * rows), F32)]
    act_copies = []
    for i, step in enumerate(steps):
        e = (me_ref[0] ^ step).astype(F32)
        prob = jnp.where(stand[:, 4:5] == e, stand[:, 0:1] + stand[:, 2:3], 0.0)
        prob = prob + jnp.where(stand[:, 5:6] == e, stand[:, 1:2] + stand[:, 3:4], 0.0)
        for copy in w_copies[i][0]:
            copy.wait()
        pre_gate = nn(x_ref[...], gu_ref[:, at(2 * i)])
        for copy in w_copies[i][1]:
            copy.wait()
        pre_up = nn(x_ref[...], gu_ref[:, at(2 * i + 1)])
        for copy in w_copies[i][2]:
            copy.wait()
        d_raw = nn(c_ref[...], down_ref[:, at(i)])
        sig = jax.nn.sigmoid(pre_gate)
        silu = pre_gate * sig
        hidden = silu * pre_up
        product = (hidden * d_raw).astype(BF16)
        sums = nt(jnp.ones((8, width), BF16), product)[0:1]
        for k in range(2):
            gates[k] = gates[k] + jnp.where(lying[4 + k : 5 + k] == e, sums, 0.0)
        d_hidden = prob * d_raw
        slope = pre_up * sig * (1.0 + pre_gate * (1.0 - sig))
        dgu_ref[:, at(2 * i)] = (d_hidden * slope).astype(BF16)
        dgu_ref[:, at(2 * i + 1)] = (d_hidden * silu).astype(BF16)
        hp_ref[:, at(i)] = (prob * hidden).astype(BF16)
        for m, source in enumerate(
            (dgu_ref.at[:, at(2 * i)], dgu_ref.at[:, at(2 * i + 1)], hp_ref.at[:, at(i)])
        ):
            for j, place in enumerate(places):
                copy = pltpu.make_async_copy(
                    source.at[j * rows : (j + 1) * rows, :],
                    act_all.at[step, m, place : place + rows, :],
                    act_sem.at[i, m, j],
                )
                copy.start()
                act_copies.append(copy)
    for copy in acc_copies:
        copy.wait()
    for side, (left, right) in enumerate(((hp_ref, down_ref), (dgu_ref, gu_ref))):
        value = nt(left[...], right[...])
        for j, out in enumerate(outs):
            part = value[j * rows : (j + 1) * rows]
            if has_acc:
                part = part + acc_refs[j][side * rows : (side + 1) * rows, :].astype(F32)
            out[side * rows : (side + 1) * rows, :] = part.astype(out.dtype)
    for j, out in enumerate(outs):
        pair = jnp.concatenate(
            [g[:, j * rows : (j + 1) * rows] for g in gates]
            + [jnp.zeros((ROUTE_ROWS - 2, rows), F32)],
            axis=0,
        )
        pair = jnp.concatenate([pair, jnp.zeros((ROUTE_ROWS, columns - rows), F32)], axis=1)
        if has_acc:
            pair = pair + acc_refs[j][2 * rows :, :].astype(F32)
        out[2 * rows :, :] = pair.astype(out.dtype)
    for copy in t_copies + act_copies:
        copy.wait()


def block(me, steps, pays, weights, accs, shared, places, *, rows, with_t, experts, tokens):
    shards, count = len(places), len(steps)
    packs = tuple(p[1] if isinstance(p, tuple) else None for p in pays)
    pays = [p[0] if isinstance(p, tuple) else p for p in pays]
    height, columns = pays[0].shape[-2:]
    width = weights[0][1].shape[2]
    total = shards * rows
    outs = [jax.ShapeDtypeStruct((height, columns), BF16)] * shards
    filled = [jax.ShapeDtypeStruct((experts, 3, tokens, width), BF16)]
    if with_t:
        filled += [jax.ShapeDtypeStruct((columns, tokens), BF16)] * 2
    old = list(shared[: len(filled)]) if shared else []
    args = list(pays) + [w for two in weights for w in two] + list(accs or []) + old
    first = 1 + len(args) - len(old)
    scratch = [pltpu.VMEM((total, columns), BF16)] * 2
    scratch += [pltpu.VMEM((columns, n * count * width), BF16) for n in (2, 1)]
    scratch += [pltpu.VMEM((total, n * count * width), BF16) for n in (2, 1)]
    if with_t:
        scratch += [pltpu.VMEM((columns, total), BF16)] * 2
    if accs:
        scratch += [pltpu.VMEM(a.shape, BF16) for a in accs]
    dma = pltpu.SemaphoreType.DMA
    scratch += [dma((count, 6)), dma((count, 3, shards)), dma((2, shards)), dma((shards,))]
    res = pl.pallas_call(
        functools.partial(
            block_kernel, tuple(steps), packs, rows, tuple(places), bool(accs), with_t, len(old)
        ),
        out_shape=outs + filled,
        in_specs=[pl.BlockSpec(memory_space=pltpu.SMEM)]
        + [VMEM] * len(pays)
        + [ANY] * (len(args) - len(pays)),
        out_specs=[VMEM] * shards + [ANY] * len(filled),
        scratch_shapes=scratch,
        input_output_aliases={first + n: shards + n for n in range(len(old))},
        compiler_params=pltpu.CompilerParams(vmem_limit_bytes=BLOCK_VMEM),
        cost_estimate=SMALL_COST,
        name="block",
    )(me, *args)
    new = list(res[shards:])
    return res[:shards], new + list(shared[len(new) :] if shared else [])


def grad_kernel(parts, count, me_ref, *refs):
    lefts = {}
    refs = list(refs)
    if parts != (2,):
        lefts[0] = lefts[1] = refs.pop(0)
    if 2 in parts:
        lefts[2] = refs.pop(0)
    for act, out in zip(refs[:count], refs[count:]):
        for n, m in enumerate(parts):
            at = m if act.shape[1] == 3 else n
            out[n] = nn(lefts[m][...], act[0, at]).astype(out.dtype)


def grad(me, experts, act_all, xt_all, ct_all, parts):
    columns, tokens = xt_all.shape
    width = act_all.shape[3]
    part = columns // 3
    lefts = ([xt_all] if parts != (2,) else []) + ([ct_all] if 2 in parts else [])
    place = parts[0] // len(parts)
    chosen = [
        pl.BlockSpec((1, len(parts), tokens, width), functools.partial(lambda r, i: (r, place, 0, 0), r))
        for r in experts
    ]
    return pl.pallas_call(
        functools.partial(grad_kernel, parts, len(experts)),
        grid=(3,),
        out_shape=[jax.ShapeDtypeStruct((len(parts), columns, width), BF16)] * len(experts),
        in_specs=[pl.BlockSpec(memory_space=pltpu.SMEM)]
        + [pl.BlockSpec((part, tokens), lambda i: (i, 0))] * len(lefts)
        + chosen,
        out_specs=[pl.BlockSpec((len(parts), part, width), lambda i: (0, i, 0))] * len(experts),
        compiler_params=pltpu.CompilerParams(vmem_limit_bytes=GRAD_VMEM),
        cost_estimate=SMALL_COST,
        name="grad",
    )(me, *lefts, *[act_all] * len(experts))


def final_kernel(places, turned, count, *refs):
    parts, outs = refs[:count], refs[count:]
    for n, out in enumerate(outs):
        value = parts[0][places[0][n]].astype(F32)
        for part, at in zip(parts[1:], places[1:]):
            value = value + part[at[n]].astype(F32)
        out[0] = value.T if turned else value


def final_sum(parts, places, turned):
    _, columns, width = parts[0].shape
    part = columns // 3
    if turned:
        shape, spec = (1, width, columns), pl.BlockSpec((1, width, part), lambda i: (0, 0, i))
    else:
        shape, spec = (1, columns, width), pl.BlockSpec((1, part, width), lambda i: (0, i, 0))
    return pl.pallas_call(
        functools.partial(final_kernel, places, turned, len(parts)),
        grid=(3,),
        out_shape=[jax.ShapeDtypeStruct(shape, F32)] * len(places[0]),
        in_specs=[pl.BlockSpec((p.shape[0], part, width), lambda i: (0, i, 0)) for p in parts],
        out_specs=[spec] * len(places[0]),
        compiler_params=pltpu.CompilerParams(vmem_limit_bytes=VMEM_LIMIT),
        cost_estimate=SMALL_COST,
        name="final",
    )(*parts)


def per_device(tokens, gate_probs, expert_ids, cotangent, gate_weight, up_weight, down_weight):
    rows, columns = tokens.shape
    experts = lax.axis_size("expert")
    inner = inner_size(lax.axis_size("fsdp"))
    outer = lax.axis_size("fsdp") // inner
    me = lax.axis_index("expert").astype(jnp.int32).reshape(1)

    high = lax.reduce_precision(gate_probs, 8, 7)
    route = jnp.concatenate([high, gate_probs - high, expert_ids.astype(F32)], axis=1).T
    route = jnp.pad(route, ((0, ROUTE_ROWS - route.shape[0]), (0, columns - rows))).astype(BF16)
    own_pay = jnp.concatenate([tokens, cotangent, route], axis=0)

    beside = lambda v: [hop(v, "fsdp", j) for j in range(1, inner)]
    near, far = [0, 1], list(range(2, experts))
    size = dict(experts=experts, tokens=outer * inner * rows, rows=rows)
    halves = lambda w: w.reshape(2, columns // 2, -1)
    turned = halves(after(down_weight[0], own_pay).T)
    own_w = [
        jnp.concatenate([halves(gate_weight[0]), halves(up_weight[0]), turned[:1]]),
        turned[1:],
    ]
    weights = {r: [None] * 2 for r in range(experts)}
    weights[0] = own_w
    pays, keep, done, shared = {}, {}, {}, None
    place = lambda k, j: (k * inner + j) * rows

    def compute(steps, shards, tick, with_t):
        nonlocal shared
        accs = None if with_t else [keep[s] for s in shards]
        packed, seen = [], {}
        for s in shards:
            p = pays[s]
            if isinstance(p, tuple):
                if id(p[0]) in seen:
                    seen[id(p[0])][1].append(p[1])
                    continue
                p = (p[0], [p[1]])
                seen[id(p[0])] = p
            packed.append(p)
        packed = [(p[0], tuple(p[1])) if isinstance(p, tuple) else p for p in packed]
        if shared:
            tick = after(me, tick, shared[0])
        outs, shared = block(
            tick, steps, packed, [weights[r] for r in steps], accs, shared,
            [place(*s) for s in shards], with_t=with_t, **size,
        )
        for s, out in zip(shards, outs):
            (done if steps[-1] == far[-1] else keep)[s] = out

    row_of = lambda k: [(k, j) for j in range(inner)]

    first = hop(own_pay, "fsdp", inner)
    second = hop(own_pay, "fsdp", 2 * inner)
    for j, p in enumerate([own_pay] + beside(own_pay)):
        pays[0, j] = p
    for r in far[::2]:
        weights[r][0] = hop(own_w[0], "expert", r)
    weights[1] = [hop(w, "expert", 1) for w in own_w]
    compute(near, row_of(0), me, True)
    gus = [weights[r][0] for r in far[::2]]
    first, second, gus, shared = lax.optimization_barrier((first, second, gus, shared))

    pays[1, 0], pays[2, 0] = first, second
    for j, p in enumerate(beside(first)):
        pays[1, j + 1] = p
    third = hop(second, "fsdp", inner)
    for r, gu in zip(far[::2], gus):
        weights[r][0] = gu
        weights[r + 1][0] = hop(gu, "expert", 1)
        weights[r][1] = hop(after(own_w[1], gu), "expert", r)
    split = inner == 2
    if split:
        compute(near, [(1, 0), (2, 0)], me, True)
    downs = [weights[r][1] for r in far[::2]]
    gus = [weights[r + 1][0] for r in far[::2]]
    firsts = [pays[1, j] for j in range(1, inner)]
    third, firsts, downs, gus, shared = lax.optimization_barrier((third, firsts, downs, gus, shared))
    for r, gu, down in zip(far[::2], gus, downs):
        weights[r][1] = down
        weights[r + 1] = [gu, hop(down, "expert", 1)]

    for j in range(1, inner):
        pays[1, j] = firsts[j - 1]
    thirds = [third] + beside(third)
    compute(far, row_of(0) + [(1, 0), (2, 0)] if split else row_of(0), me, False)
    thirds, shared, second = lax.optimization_barrier((thirds, shared, second))
    for j, p in enumerate(thirds):
        pays[3, j] = p
    for j, p in enumerate(beside(second)):
        pays[2, j + 1] = p
    compute(near + far, row_of(3), me, True)
    if split:
        compute(near + far, [(1, 1), (2, 1)], me, True)
    else:
        for k in (1, 2):
            compute(near + far, row_of(k), me, True)

    small = lambda v: v.astype(BF16)

    def join(k, got):
        total = done[k, 0].astype(F32)
        for g in got:
            total = total + g.astype(F32)
        return total

    def sends(k, *earlier):
        return [
            hop(after(done[k, j], *earlier) if earlier else done[k, j], "fsdp", j)
            for j in range(1, inner)
        ]

    act_all, xt_all, ct_all = shared
    back2, back3 = sends(2), sends(3)
    order = far[::-1]
    far_down = dict(zip(order, grad(after(me, act_all), order, act_all, xt_all, ct_all, (2,))))
    other_down = [hop(far_down[r + 1], "expert", 1) for r in far[::2]]
    tick = after(me, [far_down[r] for r in far])
    far_gu = dict(zip(order, grad(tick, order, act_all, xt_all, ct_all, (0, 1))))
    other_gu = [hop(far_gu[r + 1], "expert", 1) for r in far[::2]]
    other_down, back2, back3 = lax.optimization_barrier(
        (other_down, back2, back3, [far_gu[r] for r in far])
    )[:3]
    arrived_down, arrived_gu = [], []
    for r, other in zip(far[::2], other_down):
        chip = small(far_down[r].astype(F32) + other.astype(F32))
        arrived_down.append(hop(chip, "expert", r))
    back1 = sends(1, back2, chip)
    sum3 = small(join(3, after(back3, chip)))
    up3 = hop(sum3, "fsdp", inner)
    near_grads = grad(after(me, sum3), near[::-1], act_all, xt_all, ct_all, (0, 1, 2))
    other_gu = after(other_gu, near_grads)
    chips = [
        small(far_gu[r].astype(F32) + other.astype(F32)) for r, other in zip(far[::2], other_gu)
    ]
    up3, back1, arrived_down, chips, near_grads = lax.optimization_barrier(
        (up3, back1, arrived_down, chips, near_grads)
    )
    arrived_gu = [hop(chip, "expert", r) for r, chip in zip(far[::2], chips)]
    other_near = hop(near_grads[0], "expert", 1)
    sum2 = small(join(2, back2 + [up3]))
    home2 = hop(sum2, "fsdp", 2 * inner)
    sum1 = small(join(1, after(back1, sum2)))
    home1 = hop(sum1, "fsdp", inner)
    back0 = sends(0, sum1)
    chip = small(near_grads[1].astype(F32) + other_near.astype(F32))
    (down,) = final_sum([chip] + arrived_down, [(2,)] + [(0,)] * len(arrived_down), True)
    sum0 = join(0, after(back0, down))
    for got in (home1, home2):
        sum0 = sum0 + got.astype(F32)
    mixed, d_tokens = small(sum0[:rows]), small(sum0[rows : 2 * rows])
    d_gates = sum0[2 * rows : 2 * rows + 2, :rows].T
    gate, up = final_sum([chip] + arrived_gu, [(0, 1)] * (1 + len(arrived_gu)), False)
    return mixed, d_tokens, d_gates, gate, up, down


def solution(mesh):
    tok = P(("expert", "fsdp"), None)
    col = P("expert", None, "fsdp")
    row = P("expert", "fsdp", None)
    return jax.shard_map(
        per_device,
        mesh=mesh,
        in_specs=(tok, tok, tok, tok, col, col, row),
        out_specs=(tok, tok, tok, col, col, row),
        check_vma=False,
    )
```
